32 devices in a mesh: pipe: 2 (over core), tensor: 4 (over z), dp: 4 (over y, x).
Axes of the slice: x: 2, y: 2, z: 4, core: 2. Of those that a mesh axis runs over, the one named last changes fastest.
Arguments:
- cotangent: bfloat16 [2, 2048, 8192], P(None, 'dp', 'tensor'), may hold values from -6 to 6
- saved_short: bfloat16 [2, 2, 2048, 8192], P('pipe', None, 'dp', 'tensor'), may hold values from -3.5 to 3.5
- saved_medium: bfloat16 [2, 2, 2048, 8192], P('pipe', None, 'dp', 'tensor'), may hold values from -3.5 to 3.5
- out_weight: bfloat16 [2, 8192, 8192], P('pipe', 'tensor'), may hold values from -0.0625 to 0.0625
- short_filter: float32 [2, 7, 8192], P('pipe', None, 'tensor'), may hold values from -2.5 to 2.5
- medium_filter: float32 [2, 128, 8192], P('pipe', None, 'tensor'), may hold values from -0.5 to 0.5
- proj_in: bfloat16 [2, 8192, 64], P('pipe', 'tensor'), may hold values from -0.0625 to 0.0625
- proj_out: bfloat16 [2, 8192, 64], P('pipe'), may hold values from -0.0625 to 0.0625
Outputs:
- proj_grads: float32 [2, 2, 64, 64], P('pipe')
The draws below stay inside these ranges and needn't reach their ends.
All inputs are finite; a program needn't handle non-finite values.
Results may differ from the reference program's by a relative error of at most 0.0041.
Values may be sent and summed in bfloat16 or wider, within the bound.
A program may use at most 192 MiB of HBM per device.

```python
import math
import jax
import jax.numpy as jnp
from jax import lax

D = 8192
RANK = 64
SHORT_TAPS = 7
MED_TAPS = 128
MICRO = 2
LAYERS = 2
SEQ = 2048


def steps_of(key, shape, cuts, least, high):
    def one(dim, shards_of):
        draws = jax.random.uniform(jax.random.fold_in(jax.random.fold_in(key, 6), dim), (shards_of,), jnp.float32, least / len(cuts), high / len(cuts))
        return jnp.repeat(jnp.exp(draws), shape[dim] // shards_of).reshape((-1,) + (1,) * (len(shape) - dim - 1))

    level = one(*cuts[0])
    for cut in cuts[1:]:
        level = level * one(*cut)
    return level


def centred(own_key, dims, scale, most, split=(), kind=jnp.bfloat16):
    values = jax.random.normal(own_key, dims, jnp.float32) * scale
    if len(split) > 0:
        values = steps_of(own_key, dims, split, -0.22, 0.18) * values
    return jnp.clip(values, min=-most, max=most).astype(kind)


def setup_inputs(seed: int = 0) -> dict:
    seeds = jax.random.split(jax.random.key(seed), 9)
    return {
        "cotangent": centred(seeds[0], (MICRO, SEQ, D), 1.0, 6.0, ((1, 4), (2, 4))),
        "saved_short": centred(seeds[1], (LAYERS, MICRO, SEQ, D), 0.6, 3.5, ((0, 2), (2, 4), (3, 4))),
        "saved_medium": centred(seeds[2], (LAYERS, MICRO, SEQ, D), 0.6, 3.5, ((0, 2), (2, 4), (3, 4))),
        "out_weight": centred(seeds[3], (LAYERS, D, D), D ** -0.5, 0.0625, ((0, 2), (1, 4))),
        "short_filter": centred(seeds[4], (LAYERS, SHORT_TAPS, D), 0.4, 2.5, ((0, 2), (2, 4)), jnp.float32),
        "medium_filter": centred(seeds[5], (LAYERS, MED_TAPS, D), 0.09, 0.5, ((0, 2), (2, 4)), jnp.float32),
        "proj_in": centred(seeds[6], (LAYERS, D, RANK), D ** -0.5, 0.0625, ((0, 2), (1, 4))),
        "proj_out": centred(seeds[7], (LAYERS, D, RANK), D ** -0.5, 0.0625, ((0, 2),)),
    }


def adjoint_filter(values, filter_taps):
    tap_count = filter_taps.shape[0]
    length = values.shape[1]
    padded = jnp.pad(values, ((0, 0), (0, tap_count - 1), (0, 0)))

    def add_tap(tap_index, total):
        offset = jnp.asarray(tap_index).astype(jnp.int32)
        window = lax.dynamic_slice_in_dim(padded, offset, length, 1)
        coefficient = lax.dynamic_index_in_dim(filter_taps, offset, 0, keepdims=False)
        return total + coefficient * window
    return lax.fori_loop(0, tap_count, add_tap, jnp.zeros_like(values))

def reference(cotangent, saved_short, saved_medium, out_weight, short_filter, medium_filter, proj_in, proj_out):
    gradient = cotangent
    norm_factor = 1.0 / math.sqrt(SEQ)
    results = []
    for layer_index in range(LAYERS - 1, -1, -1):
        short_act = saved_short[layer_index].astype(jnp.float32)
        medium_act = saved_medium[layer_index].astype(jnp.float32)
        gated = (short_act * medium_act).astype(jnp.bfloat16)
        flat_grad = gradient.reshape(MICRO * SEQ, D)
        back_low = jnp.dot(flat_grad, out_weight[layer_index].T, preferred_element_type=jnp.float32).astype(jnp.bfloat16)
        back_low = lax.optimization_barrier(back_low)
        back_grad = back_low.astype(jnp.float32).reshape(MICRO, SEQ, D)
        gate_short = back_grad * medium_act
        gate_medium = back_grad * short_act
        in_side = jnp.dot(gated.reshape(MICRO * SEQ, D), proj_in[layer_index], preferred_element_type=jnp.float32).reshape(MICRO, SEQ, RANK)
        out_side = jnp.dot(flat_grad, proj_out[layer_index], preferred_element_type=jnp.float32).reshape(MICRO, SEQ, RANK)
        results.append(jnp.einsum('mtr,mtq->mrq', in_side, out_side, precision=lax.Precision.HIGHEST) * norm_factor)
        adj_short = adjoint_filter(gate_short, short_filter[layer_index])
        adj_medium = adjoint_filter(gate_medium, medium_filter[layer_index])
        gradient = (gradient.astype(jnp.float32) + adj_short + adj_medium).astype(jnp.bfloat16)
    return jnp.stack(results[::-1])
```

```python
import functools
import math

import jax
import jax.numpy as jnp
import numpy as np
from jax import lax
from jax.experimental import pallas as pl
from jax.experimental.pallas import tpu as pltpu
from jax.sharding import PartitionSpec as P

MESH = pl.DeviceIdType.MESH
BLOCK = 256
NT = (((1,), (1,)), ((), ()))


def passed_along(array, axis, by):
    devices = lax.axis_size(axis)
    pairs = [(i, i + by) for i in range(devices) if 0 <= i + by < devices]
    return lax.ppermute(array, axis, pairs)


def transforms(taps):
    size = BLOCK + taps
    freq = 2.0 * np.pi * (np.arange(size // 2) + 0.5) / size

    def table(times, sign):
        angle = freq[:, None] * times[None, :]
        return np.concatenate([np.cos(angle), sign * np.sin(angle)], axis=0)

    ahead = table(np.arange(BLOCK), -1.0).astype(jnp.bfloat16)
    filters = table(np.arange(taps), 1.0).astype(np.float32)
    back = (table(np.arange(-taps, BLOCK), -1.0) * (2.0 / size)).astype(np.float32)
    return ahead, filters, back


def kernel(
    n, parts, tile,
    x_hbm, w_hbm, ss_hbm, sm_hbm, po_hbm, fm_ref, fs_ref, ahead_ref, ftab_ref,
    z_ref, oc_ref,
    held, acc, wbuf, ss, sm, p0, p1, spec, xs, ws, ls, send_l, send_r, recv, psend, precv,
):
    z = lax.axis_index("tensor")
    top = lax.axis_index("pipe") == lax.axis_size("pipe") - 1
    has_left, has_right = z > 0, z < n - 1
    rows, depth = held.shape[1], held.shape[2]
    width = x_hbm.shape[1]
    half = spec.shape[1]
    tiles = spec.shape[2] // tile
    barrier = pltpu.get_barrier_semaphore()
    po_rows = pl.ds(pl.multiple_of(z * width, width), width)

    p0_copy = pltpu.make_async_remote_copy(
        src_ref=po_hbm.at[po_rows], dst_ref=p0, send_sem=psend, recv_sem=precv,
        device_id={"pipe": 1}, device_id_type=MESH,
    )

    def to_left(i):
        return pltpu.make_async_remote_copy(
            src_ref=held.at[i], dst_ref=held.at[i], send_sem=send_l.at[i], recv_sem=recv.at[i],
            device_id={"tensor": z - 1}, device_id_type=MESH,
        )

    def to_right(i):
        return pltpu.make_async_remote_copy(
            src_ref=held.at[i], dst_ref=held.at[i], send_sem=send_r.at[i], recv_sem=recv.at[i],
            device_id={"tensor": z + 1}, device_id_type=MESH,
        )

    def own_copy(q):
        return pltpu.make_async_copy(
            x_hbm.at[:, pl.ds(pl.multiple_of(q * depth, depth), depth)], held.at[z * parts + q], xs.at[q]
        )

    def weight_copy(i, side):
        return pltpu.make_async_copy(
            w_hbm.at[:, pl.ds(pl.multiple_of(i * depth, depth), depth)], wbuf.at[side], ws.at[side]
        )

    def multiply(i, side):
        @pl.loop(0, tiles)
        def _(c):
            weights = wbuf[side, pl.ds(pl.multiple_of(c * tile, tile), tile), :]
            acc[c] += lax.dot_general(held[i], weights, NT, preferred_element_type=jnp.float32)

    @pl.when(jnp.logical_not(top))
    def _():
        z_ref[...] = jnp.zeros_like(z_ref)
        oc_ref[...] = jnp.zeros_like(oc_ref)
        pl.semaphore_wait(barrier, 1)
        p0_copy.start()
        p0_copy.wait_send()

    @pl.when(top)
    def _():
        for q in range(parts):
            own_copy(q).start()
        saved_copies = (
            pltpu.make_async_copy(ss_hbm, ss, ls.at[0]),
            pltpu.make_async_copy(sm_hbm, sm, ls.at[1]),
        )
        p1_copy = pltpu.make_async_copy(po_hbm.at[po_rows], p1, ls.at[2])
        pl.semaphore_signal(barrier, inc=1, device_id={"pipe": 0}, device_id_type=MESH)

        @pl.when(has_left)
        def _():
            pl.semaphore_signal(barrier, inc=1, device_id={"tensor": z - 1}, device_id_type=MESH)

        @pl.when(has_right)
        def _():
            pl.semaphore_signal(barrier, inc=1, device_id={"tensor": z + 1}, device_id_type=MESH)

        pl.semaphore_wait(barrier, jnp.minimum(z, 1) + jnp.minimum(n - 1 - z, 1))

        for q in range(parts):
            own_copy(q).wait()

            @pl.when(has_left)
            def _():
                to_left(z * parts + q).start()

            @pl.when(has_right)
            def _():
                to_right(z * parts + q).start()

        p1_copy.start()
        for copy in saved_copies:
            copy.start()
        z_ref[...] = jnp.zeros_like(z_ref)
        oc_ref[...] = jnp.zeros_like(oc_ref)
        acc[...] = jnp.zeros_like(acc)

        @pl.loop(0, tiles)
        def _(c):
            cols = pl.ds(pl.multiple_of(c * tile, tile), tile)
            spec[0:2, :, cols] = jnp.dot(
                ftab_ref[...], fm_ref[:, cols], precision=lax.Precision.HIGHEST,
                preferred_element_type=jnp.float32,
            ).reshape(2, half, tile)
            for part in range(2):
                total = jnp.zeros((half, tile), jnp.float32)
                for j in range(fs_ref.shape[0]):
                    total += ftab_ref[part * half : (part + 1) * half, j : j + 1] * fs_ref[j : j + 1, cols]
                spec[2 + part, :, cols] = total

        p1_copy.wait()
        p0_copy.wait_recv()

        @pl.loop(0, parts)
        def _(q):
            i = z * parts + q
            weight_copy(i, 0).start()
            mine = pl.ds(pl.multiple_of(q * depth, depth), depth)
            oc_ref[0] += jnp.dot(held[i], p0[mine, :], preferred_element_type=jnp.float32)
            oc_ref[1] += jnp.dot(held[i], p1[mine, :], preferred_element_type=jnp.float32)
            weight_copy(i, 0).wait()
            multiply(i, 0)

        @pl.loop(1, n)
        def _(k):
            from_left, from_right = z >= k, z + k < n

            @pl.loop(0, parts)
            def _(q):
                i_left, i_right = (z - k) * parts + q, (z + k) * parts + q

                @pl.when(from_left)
                def _():
                    weight_copy(i_left, 0).start()

                @pl.when(from_right)
                def _():
                    weight_copy(i_right, 1).start()

                @pl.when(from_left)
                def _():
                    to_right(i_left).wait_recv()

                    @pl.when(has_right)
                    def _():
                        to_right(i_left).start()

                @pl.when(from_right)
                def _():
                    to_left(i_right).wait_recv()

                    @pl.when(has_left)
                    def _():
                        to_left(i_right).start()

                @pl.when(from_left)
                def _():
                    weight_copy(i_left, 0).wait()
                    multiply(i_left, 0)

                @pl.when(from_right)
                def _():
                    weight_copy(i_right, 1).wait()
                    multiply(i_right, 1)

        for copy in saved_copies:
            copy.wait()

        @pl.loop(0, tiles)
        def _(c):
            cols = pl.ds(pl.multiple_of(c * tile, tile), tile)
            for b in range(rows // BLOCK):
                span = slice(b * BLOCK, (b + 1) * BLOCK)
                back = acc[c, span, :].astype(jnp.bfloat16).astype(jnp.float32)
                gate_medium = (back * ss[span, cols].astype(jnp.float32)).astype(jnp.bfloat16)
                gate_short = (back * sm[span, cols].astype(jnp.float32)).astype(jnp.bfloat16)
                gm = jnp.dot(ahead_ref[...], gate_medium, preferred_element_type=jnp.float32)
                gs = jnp.dot(ahead_ref[...], gate_short, preferred_element_type=jnp.float32)
                m_re, m_im = spec[0, :, cols], spec[1, :, cols]
                s_re, s_im = spec[2, :, cols], spec[3, :, cols]
                real = m_re * gm[:half] - m_im * gm[half:] + s_re * gs[:half] - s_im * gs[half:]
                imag = m_re * gm[half:] + m_im * gm[:half] + s_re * gs[half:] + s_im * gs[:half]
                basis = p0[cols, :]
                base = 2 * half * b
                z_ref[base : base + half, :] += jnp.dot(
                    real.astype(jnp.bfloat16), basis, preferred_element_type=jnp.float32
                )
                z_ref[base + half : base + 2 * half, :] += jnp.dot(
                    imag.astype(jnp.bfloat16), basis, preferred_element_type=jnp.float32
                )

        @pl.loop(0, n)
        def _(s):
            @pl.loop(0, parts)
            def _(q):
                i = s * parts + q

                @pl.when(jnp.logical_and(has_left, s >= z))
                def _():
                    to_left(i).wait_send()

                @pl.when(jnp.logical_and(has_right, s <= z))
                def _():
                    to_right(i).wait_send()


def back_pass(x, weight, ss, sm, basis, fm, fs, ahead, ftab):
    n = lax.axis_size("tensor")
    rows, width = x.shape
    channels = weight.shape[0]
    rank = basis.shape[1]
    depth = min(512, width)
    parts = width // depth
    tile = min(256, channels)
    size = ahead.shape[0]
    any_spec = pl.BlockSpec(memory_space=pl.ANY)
    vmem = pl.BlockSpec(memory_space=pltpu.VMEM)
    dma = pltpu.SemaphoreType.DMA
    return pl.pallas_call(
        functools.partial(kernel, n, parts, tile),
        out_shape=(
            jax.ShapeDtypeStruct((rows // BLOCK * size, rank), jnp.float32),
            jax.ShapeDtypeStruct((2, rows, rank), jnp.float32),
        ),
        in_specs=[any_spec] * 5 + [vmem] * 4,
        out_specs=(vmem, vmem),
        scratch_shapes=[
            pltpu.VMEM((n * parts, rows, depth), jnp.bfloat16),
            pltpu.VMEM((channels // tile, rows, tile), jnp.float32),
            pltpu.VMEM((2, channels, depth), jnp.bfloat16),
            pltpu.VMEM((rows, channels), jnp.bfloat16),
            pltpu.VMEM((rows, channels), jnp.bfloat16),
            pltpu.VMEM((width, rank), jnp.bfloat16),
            pltpu.VMEM((width, rank), jnp.bfloat16),
            pltpu.VMEM((4, size // 2, channels), jnp.float32),
            dma((parts,)), dma((2,)), dma((3,)),
            dma((n * parts,)), dma((n * parts,)), dma((n * parts,)),
            dma, dma,
        ],
        cost_estimate=pl.CostEstimate(
            flops=2 * rows * channels * width * n, bytes_accessed=2 * channels * width * n, transcendentals=0
        ),
        compiler_params=pltpu.CompilerParams(
            collective_id=0, has_side_effects=True, vmem_limit_bytes=60 * 2**20
        ),
        name="back_pass",
    )(x, weight, ss, sm, basis, fm, fs, ahead, ftab)


def body(
    cotangent, saved_short, saved_medium, out_weight, short_filter, medium_filter, proj_in, proj_out
):
    section = lax.axis_index("pipe")
    micro, seq_dev, width = cotangent.shape
    rows = micro * seq_dev
    rank = proj_in.shape[2]
    norm_factor = 1.0 / math.sqrt(seq_dev * lax.axis_size("dp"))
    taps = medium_filter.shape[1]
    ahead, ftab, back = transforms(taps)
    ss = saved_short.reshape(rows, -1)
    sm = saved_medium.reshape(rows, -1)

    spectra, out_parts = back_pass(
        cotangent.reshape(rows, width), out_weight[0], ss, sm, proj_out[0],
        medium_filter[0], short_filter[0], jnp.asarray(ahead), jnp.asarray(ftab),
    )

    gated = (ss.astype(jnp.float32) * sm.astype(jnp.float32)).astype(jnp.bfloat16)
    in_part = jnp.dot(gated, proj_in[0], preferred_element_type=jnp.float32)
    in_side = lax.psum(in_part, "tensor").reshape(micro, seq_dev, rank)
    before = passed_along(in_side[:, seq_dev - taps :], "dp", 1)
    below = passed_along(jnp.concatenate([before, in_side], axis=1), "pipe", 1)
    windows = jnp.stack(
        [below[:, b * BLOCK : (b + 1) * BLOCK + taps] for b in range(seq_dev // BLOCK)], axis=1
    )
    high = lax.Precision.HIGHEST
    turned = jnp.einsum("kt,mbtr->mbkr", jnp.asarray(back), windows, precision=high)

    spectra = spectra.reshape(micro, seq_dev // BLOCK, -1, rank)
    out_parts = out_parts.reshape(2, micro, seq_dev, rank)
    lower = jnp.einsum("mbkr,mbkq->mrq", turned, spectra, precision=high)
    lower += jnp.einsum("mtr,mtq->mrq", below[:, taps:], out_parts[0], precision=high)
    upper = jnp.einsum("mtr,mtq->mrq", in_side, out_parts[1], precision=high)
    both = lax.psum(jnp.stack([lower, upper]) * norm_factor, ("pipe", "tensor", "dp"))
    return lax.dynamic_index_in_dim(both, section, 0, keepdims=True)


def solution(mesh):
    in_specs = (
        P(None, "dp", "tensor"),
        P("pipe", None, "dp", "tensor"),
        P("pipe", None, "dp", "tensor"),
        P("pipe", "tensor", None),
        P("pipe", None, "tensor"),
        P("pipe", None, "tensor"),
        P("pipe", "tensor", None),
        P("pipe", None, None),
    )
    out_specs = P("pipe", None, None, None)
    return jax.shard_map(body, mesh=mesh, in_specs=in_specs, out_specs=out_specs, check_vma=False)
```

```python
import functools
import math

import jax
import jax.numpy as jnp
import numpy as np
from jax import lax
from jax.experimental import pallas as pl
from jax.experimental.pallas import tpu as pltpu
from jax.sharding import PartitionSpec as P

MESH = pl.DeviceIdType.MESH
BLOCK = 256
NT = (((1,), (1,)), ((), ()))


def transforms(taps):
    size = BLOCK + taps
    freq = 2.0 * np.pi * (np.arange(size // 2) + 0.5) / size

    def table(times, sign):
        angle = freq[:, None] * times[None, :]
        return np.concatenate([np.cos(angle), sign * np.sin(angle)], axis=0)

    ahead = table(np.arange(BLOCK), -1.0).astype(jnp.bfloat16)
    filters = table(np.arange(taps), 1.0).astype(np.float32)
    back = (table(np.arange(-taps, BLOCK), -1.0) * (2.0 / size)).astype(np.float32)
    return ahead, filters, back


def kernel(
    n, parts, tile,
    x_hbm, w_hbm, ss_hbm, sm_hbm, po_hbm, pi_ref, fm_ref, fs_ref, ahead_ref, ftab_ref, back_ref,
    out_ref,
    held, acc, wbuf, ss, sm, p0, p1, spec, z_ref, oc_ref,
    in_own, in_sum, in_low, in_up, in_pad, turned, lower, upper, red_dp, red_z, final,
    xs, ws, ls, send_l, send_r, recv, psend, precv,
    in_send, low_recv, up_recv, halo_send, halo_recv,
    dp_send, dp_recv, z_send, z_recv, fin_send, fin_recv,
):
    z = lax.axis_index("tensor")
    y = lax.axis_index("dp")
    dps = red_dp.shape[0]
    micro, rank, padded = in_pad.shape
    taps = padded - held.shape[1] // micro
    seq = padded - taps
    scale = 1.0 / math.sqrt(seq * dps)
    high = lax.Precision.HIGHEST
    top = lax.axis_index("pipe") == lax.axis_size("pipe") - 1
    has_left, has_right = z > 0, z < n - 1
    rows, depth = held.shape[1], held.shape[2]
    width = x_hbm.shape[1]
    half = spec.shape[1]
    tiles = spec.shape[2] // tile
    barrier = pltpu.get_barrier_semaphore()
    po_rows = pl.ds(pl.multiple_of(z * width, width), width)

    p0_copy = pltpu.make_async_remote_copy(
        src_ref=po_hbm.at[:, po_rows], dst_ref=p0, send_sem=psend, recv_sem=precv,
        device_id={"pipe": 1}, device_id_type=MESH,
    )

    def to_left(i):
        return pltpu.make_async_remote_copy(
            src_ref=held.at[i], dst_ref=held.at[i], send_sem=send_l.at[i], recv_sem=recv.at[i],
            device_id={"tensor": z - 1}, device_id_type=MESH,
        )

    def to_right(i):
        return pltpu.make_async_remote_copy(
            src_ref=held.at[i], dst_ref=held.at[i], send_sem=send_r.at[i], recv_sem=recv.at[i],
            device_id={"tensor": z + 1}, device_id_type=MESH,
        )

    def own_copy(q):
        return pltpu.make_async_copy(
            x_hbm.at[:, pl.ds(pl.multiple_of(q * depth, depth), depth)], held.at[z * parts + q], xs.at[q]
        )

    def weight_copy(i, side):
        return pltpu.make_async_copy(
            w_hbm.at[:, pl.ds(pl.multiple_of(i * depth, depth), depth)], wbuf.at[side], ws.at[side]
        )

    def multiply(i, side):
        @pl.loop(0, tiles)
        def _(c):
            weights = wbuf[side, pl.ds(pl.multiple_of(c * tile, tile), tile), :]
            acc[c] += lax.dot_general(held[i], weights, NT, preferred_element_type=jnp.float32)

    saved_copies = (
        pltpu.make_async_copy(ss_hbm, ss, ls.at[0]),
        pltpu.make_async_copy(sm_hbm, sm, ls.at[1]),
    )

    def in_part():
        in_sum[...] = jnp.zeros_like(in_sum)

        @pl.loop(0, tiles)
        def _(c):
            cols = pl.ds(pl.multiple_of(c * tile, tile), tile)
            gated = (ss[:, cols].astype(jnp.float32) * sm[:, cols].astype(jnp.float32)).astype(jnp.bfloat16)
            in_sum[...] += lax.dot_general(pi_ref[:, cols], gated, NT, preferred_element_type=jnp.float32)

        in_own[...] = in_sum[...].astype(jnp.bfloat16)

    def low_copy(peer):
        return pltpu.make_async_remote_copy(
            src_ref=in_own, dst_ref=in_low.at[z], send_sem=in_send.at[peer], recv_sem=low_recv.at[z],
            device_id={"pipe": 1, "tensor": peer}, device_id_type=MESH,
        )

    def up_copy(peer):
        return pltpu.make_async_remote_copy(
            src_ref=in_own, dst_ref=in_up.at[z], send_sem=in_send.at[peer], recv_sem=up_recv.at[z],
            device_id={"tensor": peer}, device_id_type=MESH,
        )

    def arrived(slots, sems, s):
        pltpu.make_async_copy(slots.at[s], slots.at[s], sems.at[s]).wait()

    def halo_copy():
        return pltpu.make_async_remote_copy(
            src_ref=in_pad.at[:, :, pl.ds(seq, taps)], dst_ref=in_pad.at[:, :, pl.ds(0, taps)],
            send_sem=halo_send, recv_sem=halo_recv, device_id={"dp": y + 1}, device_id_type=MESH,
        )

    def dp_copy(peer):
        return pltpu.make_async_remote_copy(
            src_ref=red_dp.at[y], dst_ref=red_dp.at[y], send_sem=dp_send.at[peer], recv_sem=dp_recv.at[y],
            device_id={"dp": peer}, device_id_type=MESH,
        )

    def z_copy(peer):
        return pltpu.make_async_remote_copy(
            src_ref=red_z.at[z], dst_ref=red_z.at[z], send_sem=z_send.at[peer], recv_sem=z_recv.at[z],
            device_id={"tensor": peer}, device_id_type=MESH,
        )

    fin_copy = pltpu.make_async_remote_copy(
        src_ref=final, dst_ref=final, send_sem=fin_send, recv_sem=fin_recv,
        device_id={"pipe": 0}, device_id_type=MESH,
    )

    def collect():
        in_sum[...] = jnp.zeros_like(in_sum)

        @pl.loop(0, n)
        def _(s):
            arrived(in_low, low_recv, s)
            in_sum[...] += in_low[s].astype(jnp.float32)

        for m in range(micro):
            in_pad[m, :, taps:] = in_sum[:, m * seq : (m + 1) * seq]

        @pl.when(y < dps - 1)
        def _():
            halo_copy().start()

        @pl.when(y == 0)
        def _():
            in_pad[:, :, :taps] = jnp.zeros((micro, rank, taps), jnp.float32)

        in_sum[...] = jnp.zeros_like(in_sum)

        @pl.loop(0, n)
        def _(s):
            @pl.when(s != z)
            def _():
                arrived(in_up, up_recv, s)

            in_sum[...] += in_up[s].astype(jnp.float32)

        for m in range(micro):
            span = slice(m * seq, (m + 1) * seq)
            upper[m] = jnp.dot(
                in_sum[:, span], oc_ref[1, span, :], precision=high, preferred_element_type=jnp.float32
            )
            lower[m] = jnp.dot(
                in_pad[m, :, taps:], oc_ref[0, span, :], precision=high, preferred_element_type=jnp.float32
            )

    def turn():
        @pl.when(y > 0)
        def _():
            halo_copy().wait_recv()

        for m in range(micro):
            for b in range(seq // BLOCK):
                turned[m * (seq // BLOCK) + b] = lax.dot_general(
                    in_pad[m, :, b * BLOCK : (b + 1) * BLOCK + taps], back_ref[...], NT,
                    precision=high, preferred_element_type=jnp.float32,
                )

    @pl.when(jnp.logical_not(top))
    def _():
        for copy in saved_copies:
            copy.start()
        pl.semaphore_signal(barrier, inc=1, device_id={"pipe": 1}, device_id_type=MESH)
        pl.semaphore_wait(barrier, n)
        p0_copy.start()
        for copy in saved_copies:
            copy.wait()
        in_part()

        @pl.loop(0, n)
        def _(s):
            low_copy(s).start()

        p0_copy.wait_send()

        @pl.loop(0, n)
        def _(s):
            low_copy(s).wait_send()

        fin_copy.wait_recv()
        out_ref[...] = final[:, :, :rank]

    @pl.when(top)
    def _():
        for q in range(parts):
            own_copy(q).start()
        p1_copy = pltpu.make_async_copy(po_hbm.at[:, po_rows], p1, ls.at[2])

        @pl.loop(0, n)
        def _(s):
            pl.semaphore_signal(barrier, inc=1, device_id={"pipe": 0, "tensor": s}, device_id_type=MESH)

            @pl.when(s != z)
            def _():
                pl.semaphore_signal(barrier, inc=1, device_id={"tensor": s}, device_id_type=MESH)

        @pl.loop(0, dps)
        def _(s):
            @pl.when(s != y)
            def _():
                pl.semaphore_signal(barrier, inc=1, device_id={"dp": s}, device_id_type=MESH)

        pl.semaphore_wait(barrier, n + dps - 1)

        for q in range(parts):
            own_copy(q).wait()

            @pl.when(has_left)
            def _():
                to_left(z * parts + q).start()

            @pl.when(has_right)
            def _():
                to_right(z * parts + q).start()

        p1_copy.start()
        for copy in saved_copies:
            copy.start()
        z_ref[...] = jnp.zeros_like(z_ref)
        oc_ref[...] = jnp.zeros_like(oc_ref)
        acc[...] = jnp.zeros_like(acc)
        for copy in saved_copies:
            copy.wait()
        in_part()
        in_up[z] = in_own[...]

        @pl.loop(0, n)
        def _(s):
            @pl.when(s != z)
            def _():
                up_copy(s).start()

        @pl.loop(0, tiles)
        def _(c):
            cols = pl.ds(pl.multiple_of(c * tile, tile), tile)
            spec[0:2, :, cols] = jnp.dot(
                ftab_ref[...], fm_ref[:, cols], precision=lax.Precision.HIGHEST,
                preferred_element_type=jnp.float32,
            ).reshape(2, half, tile)
            for part in range(2):
                total = jnp.zeros((half, tile), jnp.float32)
                for j in range(fs_ref.shape[0]):
                    total += ftab_ref[part * half : (part + 1) * half, j : j + 1] * fs_ref[j : j + 1, cols]
                spec[2 + part, :, cols] = total

        p1_copy.wait()
        p0_copy.wait_recv()

        @pl.loop(0, parts)
        def _(q):
            i = z * parts + q
            weight_copy(i, 0).start()
            mine = pl.ds(pl.multiple_of(q * depth, depth), depth)
            oc_ref[0] += lax.dot_general(held[i], p0[:, mine], NT, preferred_element_type=jnp.float32)
            oc_ref[1] += lax.dot_general(held[i], p1[:, mine], NT, preferred_element_type=jnp.float32)
            weight_copy(i, 0).wait()
            multiply(i, 0)

        @pl.loop(1, n)
        def _(k):
            from_left, from_right = z >= k, z + k < n

            @pl.when(k == max(1, n - 2))
            def _():
                collect()

            @pl.when(k == n - 1)
            def _():
                turn()

            @pl.loop(0, parts)
            def _(q):
                i_left, i_right = (z - k) * parts + q, (z + k) * parts + q

                @pl.when(from_left)
                def _():
                    weight_copy(i_left, 0).start()

                @pl.when(from_right)
                def _():
                    weight_copy(i_right, 1).start()

                @pl.when(from_left)
                def _():
                    to_right(i_left).wait_recv()

                    @pl.when(has_right)
                    def _():
                        to_right(i_left).start()

                @pl.when(from_right)
                def _():
                    to_left(i_right).wait_recv()

                    @pl.when(has_left)
                    def _():
                        to_left(i_right).start()

                @pl.when(from_left)
                def _():
                    weight_copy(i_left, 0).wait()
                    multiply(i_left, 0)

                @pl.when(from_right)
                def _():
                    weight_copy(i_right, 1).wait()
                    multiply(i_right, 1)

        @pl.loop(0, tiles)
        def _(c):
            cols = pl.ds(pl.multiple_of(c * tile, tile), tile)
            for b in range(rows // BLOCK):
                span = slice(b * BLOCK, (b + 1) * BLOCK)
                back = acc[c, span, :].astype(jnp.bfloat16).astype(jnp.float32)
                gate_medium = (back * ss[span, cols].astype(jnp.float32)).astype(jnp.bfloat16)
                gate_short = (back * sm[span, cols].astype(jnp.float32)).astype(jnp.bfloat16)
                gm = jnp.dot(ahead_ref[...], gate_medium, preferred_element_type=jnp.float32)
                gs = jnp.dot(ahead_ref[...], gate_short, preferred_element_type=jnp.float32)
                m_re, m_im = spec[0, :, cols], spec[1, :, cols]
                s_re, s_im = spec[2, :, cols], spec[3, :, cols]
                real = m_re * gm[:half] - m_im * gm[half:] + s_re * gs[:half] - s_im * gs[half:]
                imag = m_re * gm[half:] + m_im * gm[:half] + s_re * gs[half:] + s_im * gs[:half]
                basis = p0[:, cols]
                base = 2 * half * b
                z_ref[base : base + half, :] += lax.dot_general(
                    real.astype(jnp.bfloat16), basis, NT, preferred_element_type=jnp.float32
                )
                z_ref[base + half : base + 2 * half, :] += lax.dot_general(
                    imag.astype(jnp.bfloat16), basis, NT, preferred_element_type=jnp.float32
                )

        size = 2 * half
        for m in range(micro):
            total = lower[m]
            for b in range(seq // BLOCK):
                at = m * (seq // BLOCK) + b
                total += jnp.dot(
                    turned[at], z_ref[at * size : (at + 1) * size, :], precision=high,
                    preferred_element_type=jnp.float32,
                )
            red_dp[y, m] = jnp.concatenate([total, upper[m]], axis=1) * scale

        @pl.loop(0, dps)
        def _(s):
            @pl.when(s != y)
            def _():
                dp_copy(s).start()

        @pl.loop(0, dps)
        def _(s):
            @pl.when(s != y)
            def _():
                arrived(red_dp, dp_recv, s)

        total = red_dp[0]
        for s in range(1, dps):
            total += red_dp[s]
        red_z[z] = total

        @pl.loop(0, n)
        def _(s):
            @pl.when(s != z)
            def _():
                z_copy(s).start()

        @pl.loop(0, n)
        def _(s):
            @pl.when(s != z)
            def _():
                arrived(red_z, z_recv, s)

        total = red_z[0]
        for s in range(1, n):
            total += red_z[s]
        final[...] = total
        fin_copy.start()
        out_ref[...] = final[:, :, rank:]
        fin_copy.wait_send()

        @pl.when(y < dps - 1)
        def _():
            halo_copy().wait_send()

        @pl.loop(0, dps)
        def _(s):
            @pl.when(s != y)
            def _():
                dp_copy(s).wait_send()

        @pl.loop(0, n)
        def _(s):
            @pl.when(s != z)
            def _():
                z_copy(s).wait_send()
                up_copy(s).wait_send()

            @pl.loop(0, parts)
            def _(q):
                i = s * parts + q

                @pl.when(jnp.logical_and(has_left, s >= z))
                def _():
                    to_left(i).wait_send()

                @pl.when(jnp.logical_and(has_right, s <= z))
                def _():
                    to_right(i).wait_send()


def body(
    cotangent, saved_short, saved_medium, out_weight, short_filter, medium_filter, proj_in, proj_out
):
    n, dps = lax.axis_size("tensor"), lax.axis_size("dp")
    micro, seq, width = cotangent.shape
    rows = micro * seq
    channels = saved_short.shape[3]
    rank = proj_in.shape[2]
    taps = medium_filter.shape[1]
    ahead, ftab, back = transforms(taps)
    size = ahead.shape[0]
    depth = min(512, width)
    parts = width // depth
    tile = min(256, channels)
    blocks = rows // BLOCK
    any_spec = pl.BlockSpec(memory_space=pl.ANY)
    vmem = pl.BlockSpec(memory_space=pltpu.VMEM)
    dma = pltpu.SemaphoreType.DMA
    low, full = jnp.bfloat16, jnp.float32
    grads = pl.pallas_call(
        functools.partial(kernel, n, parts, tile),
        out_shape=jax.ShapeDtypeStruct((micro, rank, rank), full),
        in_specs=[any_spec] * 5 + [vmem] * 6,
        out_specs=vmem,
        scratch_shapes=[
            pltpu.VMEM((n * parts, rows, depth), low),
            pltpu.VMEM((channels // tile, rows, tile), full),
            pltpu.VMEM((2, channels, depth), low),
            pltpu.VMEM((rows, channels), low),
            pltpu.VMEM((rows, channels), low),
            pltpu.VMEM((rank, width), low),
            pltpu.VMEM((rank, width), low),
            pltpu.VMEM((4, size // 2, channels), full),
            pltpu.VMEM((blocks * size, rank), full),
            pltpu.VMEM((2, rows, rank), full),
            pltpu.VMEM((rank, rows), low),
            pltpu.VMEM((rank, rows), full),
            pltpu.VMEM((n, rank, rows), low),
            pltpu.VMEM((n, rank, rows), low),
            pltpu.VMEM((micro, rank, taps + seq), full),
            pltpu.VMEM((blocks, rank, size), full),
            pltpu.VMEM((micro, rank, rank), full),
            pltpu.VMEM((micro, rank, rank), full),
            pltpu.VMEM((dps, micro, rank, 2 * rank), full),
            pltpu.VMEM((n, micro, rank, 2 * rank), full),
            pltpu.VMEM((micro, rank, 2 * rank), full),
            dma((parts,)), dma((2,)), dma((3,)),
            dma((n * parts,)), dma((n * parts,)), dma((n * parts,)),
            dma, dma,
            dma((n,)), dma((n,)), dma((n,)), dma, dma,
            dma((dps,)), dma((dps,)), dma((n,)), dma((n,)), dma, dma,
        ],
        cost_estimate=pl.CostEstimate(
            flops=2 * rows * channels * width * n, bytes_accessed=2 * channels * width * n, transcendentals=0
        ),
        compiler_params=pltpu.CompilerParams(
            collective_id=0, has_side_effects=True, vmem_limit_bytes=60 * 2**20
        ),
        name="back_pass",
    )(
        cotangent.reshape(rows, width), out_weight[0], saved_short.reshape(rows, channels),
        saved_medium.reshape(rows, channels), proj_out[0].T, proj_in[0].T,
        medium_filter[0], short_filter[0], jnp.asarray(ahead), jnp.asarray(ftab), jnp.asarray(back),
    )
    return grads[None]


def solution(mesh):
    in_specs = (
        P(None, "dp", "tensor"),
        P("pipe", None, "dp", "tensor"),
        P("pipe", None, "dp", "tensor"),
        P("pipe", "tensor", None),
        P("pipe", None, "tensor"),
        P("pipe", None, "tensor"),
        P("pipe", "tensor", None),
        P("pipe", None, None),
    )
    out_specs = P("pipe", None, None, None)
    return jax.shard_map(body, mesh=mesh, in_specs=in_specs, out_specs=out_specs, check_vma=False)
```

```python
import functools
import math

import jax
import jax.numpy as jnp
import numpy as np
from jax import lax
from jax.experimental import pallas as pl
from jax.experimental.pallas import tpu as pltpu
from jax.sharding import PartitionSpec as P

MESH = pl.DeviceIdType.MESH
BLOCK = 256
NT = (((1,), (1,)), ((), ()))


def transforms(taps):
    size = BLOCK + taps
    freq = 2.0 * np.pi * (np.arange(size // 2) + 0.5) / size

    def table(times, sign):
        angle = freq[:, None] * times[None, :]
        return np.concatenate([np.cos(angle), sign * np.sin(angle)], axis=0)

    ahead = table(np.arange(BLOCK), -1.0).astype(jnp.bfloat16)
    filters = table(np.arange(taps), 1.0).astype(np.float32)
    back = (table(np.arange(-taps, BLOCK), -1.0) * (2.0 / size)).astype(np.float32)
    return ahead, filters, back


def kernel(
    n, tile,
    x_hbm, w_hbm, ss_hbm, sm_hbm, po_hbm, pi_ref, fm_ref, fs_ref, ahead_ref, ftab_ref, back_ref,
    out_ref,
    held, acc, wbuf, ss, sm, p0, p1, spec, z_ref, oc_ref,
    in_own, in_sum, in_low, in_up, in_pad, turned, lower, upper, red_dp, red_z, final,
    xs, ws, ls, send_l, send_r, recv, psend, precv,
    in_send, low_recv, halo_send, halo_recv,
    dp_send, dp_recv, z_send, z_recv, fin_send, fin_recv,
):
    z = lax.axis_index("tensor")
    y = lax.axis_index("dp")
    dps = red_dp.shape[0]
    micro, rank, padded = in_pad.shape
    parts, width = held.shape[1], held.shape[3]
    taps = padded - parts * BLOCK // micro
    seq = padded - taps
    scale = 1.0 / math.sqrt(seq * dps)
    high = lax.Precision.HIGHEST
    top = lax.axis_index("pipe") == lax.axis_size("pipe") - 1
    has_left, has_right = z > 0, z < n - 1
    half = spec.shape[1]
    tiles = spec.shape[2] // tile
    barrier = pltpu.get_barrier_semaphore()
    po_rows = pl.ds(pl.multiple_of(z * width, width), width)

    p0_copy = pltpu.make_async_remote_copy(
        src_ref=po_hbm.at[:, po_rows], dst_ref=p0, send_sem=psend, recv_sem=precv,
        device_id={"pipe": 1}, device_id_type=MESH,
    )

    def to_left(s, r, src=None):
        return pltpu.make_async_remote_copy(
            src_ref=held.at[s, r] if src is None else src, dst_ref=held.at[s, r],
            send_sem=send_l.at[s, r], recv_sem=recv.at[s, r],
            device_id={"tensor": z - 1}, device_id_type=MESH,
        )

    def to_right(s, r, src=None):
        return pltpu.make_async_remote_copy(
            src_ref=held.at[s, r] if src is None else src, dst_ref=held.at[s, r],
            send_sem=send_r.at[s, r], recv_sem=recv.at[s, r],
            device_id={"tensor": z + 1}, device_id_type=MESH,
        )

    def own_rows(r):
        return x_hbm.at[pl.ds(r * BLOCK, BLOCK), :]

    def own_copy(r):
        return pltpu.make_async_copy(own_rows(r), held.at[z, r], xs.at[r])

    def weight_copy(s):
        return pltpu.make_async_copy(
            w_hbm.at[:, pl.ds(pl.multiple_of(s * width, width), width)], wbuf, ws
        )

    def shard_cols(s):
        return pl.ds(pl.multiple_of(s * width, width), width)

    def multiply(s):
        weight_copy(s).start()
        shard = held[s].reshape(parts * BLOCK, width)
        oc_ref[1] += lax.dot_general(
            shard, p1[:, shard_cols(s)], NT, preferred_element_type=jnp.float32
        ).reshape(parts, BLOCK, rank)
        weight_copy(s).wait()

        @pl.loop(0, tiles)
        def _(c):
            weights = wbuf[pl.ds(pl.multiple_of(c * tile, tile), tile), :]
            acc[c] += lax.dot_general(
                held[s].reshape(parts * BLOCK, width), weights, NT, preferred_element_type=jnp.float32
            ).reshape(parts, BLOCK, tile)

    saved_copies = (
        pltpu.make_async_copy(ss_hbm, ss, ls.at[0]),
        pltpu.make_async_copy(sm_hbm, sm, ls.at[1]),
    )

    def in_part():
        in_sum[...] = jnp.zeros_like(in_sum)

        @pl.loop(0, tiles)
        def _(c):
            cols = pl.ds(pl.multiple_of(c * tile, tile), tile)
            gated = (ss[:, cols].astype(jnp.float32) * sm[:, cols].astype(jnp.float32)).astype(jnp.bfloat16)
            in_sum[...] += lax.dot_general(pi_ref[:, cols], gated, NT, preferred_element_type=jnp.float32)

    def low_copy(peer):
        return pltpu.make_async_remote_copy(
            src_ref=in_own, dst_ref=in_low.at[z], send_sem=in_send.at[peer], recv_sem=low_recv.at[z],
            device_id={"pipe": 1, "tensor": peer}, device_id_type=MESH,
        )

    def arrived(slots, sems, s):
        pltpu.make_async_copy(slots.at[s], slots.at[s], sems.at[s]).wait()

    def halo_copy():
        return pltpu.make_async_remote_copy(
            src_ref=in_pad.at[:, :, pl.ds(seq, taps)], dst_ref=in_pad.at[:, :, pl.ds(0, taps)],
            send_sem=halo_send, recv_sem=halo_recv, device_id={"dp": y + 1}, device_id_type=MESH,
        )

    def dp_copy(peer):
        return pltpu.make_async_remote_copy(
            src_ref=red_dp.at[y], dst_ref=red_dp.at[y], send_sem=dp_send.at[peer], recv_sem=dp_recv.at[y],
            device_id={"dp": peer}, device_id_type=MESH,
        )

    def z_copy(peer):
        return pltpu.make_async_remote_copy(
            src_ref=red_z.at[z], dst_ref=red_z.at[z], send_sem=z_send.at[peer], recv_sem=z_recv.at[z],
            device_id={"tensor": peer}, device_id_type=MESH,
        )

    fin_copy = pltpu.make_async_remote_copy(
        src_ref=final, dst_ref=final, send_sem=fin_send, recv_sem=fin_recv,
        device_id={"pipe": 0}, device_id_type=MESH,
    )

    def collect():
        in_sum[...] = jnp.zeros_like(in_sum)

        @pl.loop(0, n)
        def _(s):
            arrived(in_low, low_recv, s)
            in_sum[...] += in_low[s].astype(jnp.float32)

        for m in range(micro):
            in_pad[m, :, taps:] = in_sum[:, m * seq : (m + 1) * seq]

        @pl.when(y < dps - 1)
        def _():
            halo_copy().start()

        @pl.when(y == 0)
        def _():
            in_pad[:, :, :taps] = jnp.zeros((micro, rank, taps), jnp.float32)

        for m in range(micro):
            each = parts // micro
            lower[m] = jnp.dot(
                in_pad[m, :, taps:], oc_ref[0, m * each : (m + 1) * each].reshape(seq, rank),
                precision=high, preferred_element_type=jnp.float32,
            )

    def turn():
        @pl.when(y > 0)
        def _():
            halo_copy().wait_recv()

        for m in range(micro):
            for b in range(seq // BLOCK):
                turned[m * (seq // BLOCK) + b] = lax.dot_general(
                    in_pad[m, :, b * BLOCK : (b + 1) * BLOCK + taps], back_ref[...], NT,
                    precision=high, preferred_element_type=jnp.float32,
                )

    @pl.when(jnp.logical_not(top))
    def _():
        for copy in saved_copies:
            copy.start()
        pl.semaphore_signal(barrier, inc=1, device_id={"pipe": 1}, device_id_type=MESH)
        pl.semaphore_wait(barrier, n)
        p0_copy.start()
        for copy in saved_copies:
            copy.wait()
        in_part()
        in_own[...] = in_sum[...].astype(jnp.bfloat16)

        @pl.loop(0, n)
        def _(s):
            low_copy(s).start()

        p0_copy.wait_send()

        @pl.loop(0, n)
        def _(s):
            low_copy(s).wait_send()

        fin_copy.wait_recv()
        out_ref[...] = final[:, :, :rank]

    @pl.when(top)
    def _():
        for r in range(parts):
            own_copy(r).start()
        p1_copy = pltpu.make_async_copy(po_hbm, p1, ls.at[2])

        @pl.loop(0, n)
        def _(s):
            pl.semaphore_signal(barrier, inc=1, device_id={"pipe": 0, "tensor": s}, device_id_type=MESH)

            @pl.when(s != z)
            def _():
                pl.semaphore_signal(barrier, inc=1, device_id={"tensor": s}, device_id_type=MESH)

        @pl.loop(0, dps)
        def _(s):
            @pl.when(s != y)
            def _():
                pl.semaphore_signal(barrier, inc=1, device_id={"dp": s}, device_id_type=MESH)

        pl.semaphore_wait(barrier, n + dps - 1)

        for r in range(parts):
            @pl.when(has_left)
            def _():
                to_left(z, r, own_rows(r)).start()

            @pl.when(has_right)
            def _():
                to_right(z, r, own_rows(r)).start()

        p1_copy.start()
        for copy in saved_copies:
            copy.start()
        oc_ref[...] = jnp.zeros_like(oc_ref)
        upper[...] = jnp.zeros_like(upper)
        acc[...] = jnp.zeros_like(acc)
        for copy in saved_copies:
            copy.wait()
        in_part()
        in_up[...] = in_sum[...]

        @pl.loop(0, tiles)
        def _(c):
            cols = pl.ds(pl.multiple_of(c * tile, tile), tile)
            spec[0:2, :, cols] = jnp.dot(
                ftab_ref[...], fm_ref[:, cols], precision=lax.Precision.HIGHEST,
                preferred_element_type=jnp.float32,
            ).reshape(2, half, tile)
            for part in range(2):
                total = jnp.zeros((half, tile), jnp.float32)
                for j in range(fs_ref.shape[0]):
                    total += ftab_ref[part * half : (part + 1) * half, j : j + 1] * fs_ref[j, :, cols]
                spec[2 + part, :, cols] = total

        p1_copy.wait()
        p0_copy.wait_recv()
        for r in range(parts):
            own_copy(r).wait()
        oc_ref[0] = lax.dot_general(
            held[z].reshape(parts * BLOCK, width), p0[...], NT, preferred_element_type=jnp.float32
        ).reshape(parts, BLOCK, rank)
        multiply(z)
        if n < 3:
            collect()

        @pl.loop(1, n - 1)
        def _(k):
            from_left, from_right = z >= k, z + k < n

            @pl.when(k == n - 2)
            def _():
                collect()

            @pl.loop(0, parts)
            def _(r):
                @pl.when(from_left)
                def _():
                    to_right(z - k, r).wait_recv()

                    @pl.when(has_right)
                    def _():
                        to_right(z - k, r).start()

                @pl.when(from_right)
                def _():
                    to_left(z + k, r).wait_recv()

                    @pl.when(has_left)
                    def _():
                        to_left(z + k, r).start()

            @pl.when(from_left)
            def _():
                multiply(z - k)

            @pl.when(from_right)
            def _():
                multiply(z + k)

        is_end = jnp.logical_or(z == 0, z == n - 1)
        farthest = n - 1 - z

        @pl.when(is_end)
        def _():
            weight_copy(farthest).start()

        turn()

        @pl.when(is_end)
        def _():
            weight_copy(farthest).wait()

        each = parts // micro

        @pl.loop(0, parts)
        def _(r):
            @pl.when(is_end)
            def _():
                to_left(farthest, r).wait_recv()
                oc_ref[1, r] += lax.dot_general(
                    held[farthest, r], p1[:, shard_cols(farthest)], NT, preferred_element_type=jnp.float32
                )

            z_ref[...] = jnp.zeros_like(z_ref)
            span = pl.ds(pl.multiple_of(r * BLOCK, BLOCK), BLOCK)

            @pl.loop(0, tiles)
            def _(c):
                cols = pl.ds(pl.multiple_of(c * tile, tile), tile)

                @pl.when(is_end)
                def _():
                    acc[c, r] += lax.dot_general(
                        held[farthest, r], wbuf[cols, :], NT, preferred_element_type=jnp.float32
                    )

                back = acc[c, r].astype(jnp.bfloat16).astype(jnp.float32)
                gate_medium = (back * ss[span, cols].astype(jnp.float32)).astype(jnp.bfloat16)
                gate_short = (back * sm[span, cols].astype(jnp.float32)).astype(jnp.bfloat16)
                gm = jnp.dot(ahead_ref[...], gate_medium, preferred_element_type=jnp.float32)
                gs = jnp.dot(ahead_ref[...], gate_short, preferred_element_type=jnp.float32)
                m_re, m_im = spec[0, :, cols], spec[1, :, cols]
                s_re, s_im = spec[2, :, cols], spec[3, :, cols]
                real = m_re * gm[:half] - m_im * gm[half:] + s_re * gs[:half] - s_im * gs[half:]
                imag = m_re * gm[half:] + m_im * gm[:half] + s_re * gs[half:] + s_im * gs[:half]
                both = jnp.concatenate([real, imag], axis=0).astype(jnp.bfloat16)
                z_ref[...] += lax.dot_general(both, p0[:, cols], NT, preferred_element_type=jnp.float32)

            m = r // each
            lower[m] += jnp.dot(
                turned[r], z_ref[...], precision=high, preferred_element_type=jnp.float32
            )
            upper[m] += jnp.dot(
                in_up[:, span], oc_ref[1, r], precision=high, preferred_element_type=jnp.float32
            )

        for m in range(micro):
            red_dp[y, m] = jnp.concatenate([lower[m], upper[m]], axis=1) * scale

        @pl.loop(0, dps)
        def _(s):
            @pl.when(s != y)
            def _():
                dp_copy(s).start()

        @pl.loop(0, dps)
        def _(s):
            @pl.when(s != y)
            def _():
                arrived(red_dp, dp_recv, s)

        total = red_dp[0]
        for s in range(1, dps):
            total += red_dp[s]
        red_z[z] = total

        @pl.loop(0, n)
        def _(s):
            @pl.when(s != z)
            def _():
                z_copy(s).start()

        @pl.loop(0, n)
        def _(s):
            @pl.when(s != z)
            def _():
                arrived(red_z, z_recv, s)

        total = red_z[0]
        for s in range(1, n):
            total += red_z[s]
        final[...] = total
        fin_copy.start()
        out_ref[...] = final[:, :, rank:]
        fin_copy.wait_send()

        @pl.when(y < dps - 1)
        def _():
            halo_copy().wait_send()

        @pl.loop(0, dps)
        def _(s):
            @pl.when(s != y)
            def _():
                dp_copy(s).wait_send()

        @pl.loop(0, n)
        def _(s):
            @pl.when(s != z)
            def _():
                z_copy(s).wait_send()

            @pl.loop(0, parts)
            def _(r):
                @pl.when(jnp.logical_and(has_left, s >= z))
                def _():
                    to_left(s, r).wait_send()

                @pl.when(jnp.logical_and(has_right, s <= z))
                def _():
                    to_right(s, r).wait_send()


def body(
    cotangent, saved_short, saved_medium, out_weight, short_filter, medium_filter, proj_in, proj_out
):
    n, dps = lax.axis_size("tensor"), lax.axis_size("dp")
    micro, seq, width = cotangent.shape
    rows = micro * seq
    channels = saved_short.shape[3]
    rank = proj_in.shape[2]
    taps = medium_filter.shape[1]
    ahead, ftab, back = transforms(taps)
    size = ahead.shape[0]
    tile = min(256, channels)
    parts = rows // BLOCK
    any_spec = pl.BlockSpec(memory_space=pl.ANY)
    vmem = pl.BlockSpec(memory_space=pltpu.VMEM)
    dma = pltpu.SemaphoreType.DMA
    low, full = jnp.bfloat16, jnp.float32
    grads = pl.pallas_call(
        functools.partial(kernel, n, tile),
        out_shape=jax.ShapeDtypeStruct((micro, rank, rank), full),
        in_specs=[any_spec] * 5 + [vmem] * 6,
        out_specs=vmem,
        scratch_shapes=[
            pltpu.VMEM((n, parts, BLOCK, width), low),
            pltpu.VMEM((channels // tile, parts, BLOCK, tile), full),
            pltpu.VMEM((channels, width), low),
            pltpu.VMEM((rows, channels), low),
            pltpu.VMEM((rows, channels), low),
            pltpu.VMEM((rank, width), low),
            pltpu.VMEM((rank, n * width), low),
            pltpu.VMEM((4, size // 2, channels), full),
            pltpu.VMEM((size, rank), full),
            pltpu.VMEM((2, parts, BLOCK, rank), full),
            pltpu.VMEM((rank, rows), low),
            pltpu.VMEM((rank, rows), full),
            pltpu.VMEM((n, rank, rows), low),
            pltpu.VMEM((rank, rows), full),
            pltpu.VMEM((micro, rank, taps + seq), full),
            pltpu.VMEM((parts, rank, size), full),
            pltpu.VMEM((micro, rank, rank), full),
            pltpu.VMEM((micro, rank, rank), full),
            pltpu.VMEM((dps, micro, rank, 2 * rank), full),
            pltpu.VMEM((n, micro, rank, 2 * rank), full),
            pltpu.VMEM((micro, rank, 2 * rank), full),
            dma((parts,)), dma, dma((3,)),
            dma((n, parts)), dma((n, parts)), dma((n, parts)),
            dma, dma,
            dma((n,)), dma((n,)), dma, dma,
            dma((dps,)), dma((dps,)), dma((n,)), dma((n,)), dma, dma,
        ],
        cost_estimate=pl.CostEstimate(
            flops=2 * rows * channels * width * n, bytes_accessed=2 * channels * width * n, transcendentals=0
        ),
        compiler_params=pltpu.CompilerParams(
            collective_id=0, has_side_effects=True, vmem_limit_bytes=60 * 2**20
        ),
        name="back_pass",
    )(
        cotangent.reshape(rows, width), out_weight[0], saved_short.reshape(rows, channels),
        saved_medium.reshape(rows, channels), proj_out[0].T, proj_in[0].T,
        medium_filter[0], short_filter.transpose(1, 0, 2), jnp.asarray(ahead), jnp.asarray(ftab), jnp.asarray(back),
    )
    return grads[None]


def solution(mesh):
    in_specs = (
        P(None, "dp", "tensor"),
        P("pipe", None, "dp", "tensor"),
        P("pipe", None, "dp", "tensor"),
        P("pipe", "tensor", None),
        P("pipe", None, "tensor"),
        P("pipe", None, "tensor"),
        P("pipe", "tensor", None),
        P("pipe", None, None),
    )
    out_specs = P("pipe", None, None, None)
    return jax.shard_map(body, mesh=mesh, in_specs=in_specs, out_specs=out_specs, check_vma=False)
```

```python
import functools
import math

import jax
import jax.numpy as jnp
import numpy as np
from jax import lax
from jax.experimental import pallas as pl
from jax.experimental.pallas import tpu as pltpu
from jax.sharding import PartitionSpec as P

MESH = pl.DeviceIdType.MESH
BLOCK = 256
HALF = BLOCK // 2
NT = (((1,), (1,)), ((), ()))


def transforms(taps):
    size = BLOCK + taps
    freq = 2.0 * np.pi * (np.arange(size // 2) + 0.5) / size

    def table(times, sign):
        angle = freq[:, None] * times[None, :]
        return np.concatenate([np.cos(angle), sign * np.sin(angle)], axis=0)

    ahead = table(np.arange(BLOCK), -1.0).astype(jnp.bfloat16)
    filters = table(np.arange(taps), 1.0).astype(np.float32)
    back = (table(np.arange(-taps, BLOCK), -1.0) * (2.0 / size)).astype(np.float32)
    return ahead, filters, back


def kernel(
    n, tile,
    x_hbm, w_hbm, ss_hbm, sm_hbm, po_hbm, pi_ref, fm_ref, fs_ref, ahead_ref, ftab_ref, back_ref,
    out_ref,
    held, acc, wbuf, ss, sm, p0, p1, spec, z_ref, oc_ref,
    in_own, in_sum, in_low, in_up, in_pad, turned, lower, upper, red_dp, red_z, final,
    xs, ws, ls, send_l, send_r, recv, psend, precv,
    in_send, low_recv, halo_send, halo_recv,
    dp_send, dp_recv, z_send, z_recv, fin_send, fin_recv,
):
    z = lax.axis_index("tensor")
    y = lax.axis_index("dp")
    dps = red_dp.shape[0]
    micro, rank, padded = in_pad.shape
    parts, width = held.shape[1], held.shape[3]
    taps = padded - parts * BLOCK // micro
    seq = padded - taps
    scale = 1.0 / math.sqrt(seq * dps)
    high = lax.Precision.HIGHEST
    top = lax.axis_index("pipe") == lax.axis_size("pipe") - 1
    has_left, has_right = z > 0, z < n - 1
    half = spec.shape[1]
    tiles = spec.shape[2] // tile
    barrier = pltpu.get_barrier_semaphore()
    po_rows = pl.ds(pl.multiple_of(z * width, width), width)

    p0_copy = pltpu.make_async_remote_copy(
        src_ref=po_hbm.at[:, po_rows], dst_ref=p0, send_sem=psend, recv_sem=precv,
        device_id={"pipe": 1}, device_id_type=MESH,
    )

    pieces = 2 * parts

    def piece(s, g):
        return held.at[s, g // 2, pl.ds(pl.multiple_of((g % 2) * HALF, HALF), HALF), :]

    def to_left(s, g, src=None):
        return pltpu.make_async_remote_copy(
            src_ref=piece(s, g) if src is None else src, dst_ref=piece(s, g),
            send_sem=send_l.at[s, g], recv_sem=recv.at[s, g],
            device_id={"tensor": z - 1}, device_id_type=MESH,
        )

    def to_right(s, g, src=None):
        return pltpu.make_async_remote_copy(
            src_ref=piece(s, g) if src is None else src, dst_ref=piece(s, g),
            send_sem=send_r.at[s, g], recv_sem=recv.at[s, g],
            device_id={"tensor": z + 1}, device_id_type=MESH,
        )

    def own_piece(g):
        return x_hbm.at[pl.ds(g * HALF, HALF), :]

    def own_copy(r):
        return pltpu.make_async_copy(x_hbm.at[pl.ds(r * BLOCK, BLOCK), :], held.at[z, r], xs.at[r])

    def weight_copy(s):
        return pltpu.make_async_copy(
            w_hbm.at[:, pl.ds(pl.multiple_of(s * width, width), width)], wbuf, ws
        )

    def shard_cols(s):
        return pl.ds(pl.multiple_of(s * width, width), width)

    def multiply(s):
        weight_copy(s).start()
        shard = held[s].reshape(parts * BLOCK, width)
        oc_ref[1] += lax.dot_general(
            shard, p1[:, shard_cols(s)], NT, preferred_element_type=jnp.float32
        ).reshape(parts, BLOCK, rank)
        weight_copy(s).wait()

        @pl.loop(0, tiles)
        def _(c):
            weights = wbuf[pl.ds(pl.multiple_of(c * tile, tile), tile), :]
            acc[c] += lax.dot_general(
                held[s].reshape(parts * BLOCK, width), weights, NT, preferred_element_type=jnp.float32
            ).reshape(parts, BLOCK, tile)

    saved_copies = (
        pltpu.make_async_copy(ss_hbm, ss, ls.at[0]),
        pltpu.make_async_copy(sm_hbm, sm, ls.at[1]),
    )

    def in_part():
        in_sum[...] = jnp.zeros_like(in_sum)

        @pl.loop(0, tiles)
        def _(c):
            cols = pl.ds(pl.multiple_of(c * tile, tile), tile)
            gated = (ss[:, cols].astype(jnp.float32) * sm[:, cols].astype(jnp.float32)).astype(jnp.bfloat16)
            in_sum[...] += lax.dot_general(pi_ref[:, cols], gated, NT, preferred_element_type=jnp.float32)

    def low_copy(peer):
        return pltpu.make_async_remote_copy(
            src_ref=in_own, dst_ref=in_low.at[z], send_sem=in_send.at[peer], recv_sem=low_recv.at[z],
            device_id={"pipe": 1, "tensor": peer}, device_id_type=MESH,
        )

    def arrived(slots, sems, s):
        pltpu.make_async_copy(slots.at[s], slots.at[s], sems.at[s]).wait()

    def halo_copy():
        return pltpu.make_async_remote_copy(
            src_ref=in_pad.at[:, :, pl.ds(seq, taps)], dst_ref=in_pad.at[:, :, pl.ds(0, taps)],
            send_sem=halo_send, recv_sem=halo_recv, device_id={"dp": y + 1}, device_id_type=MESH,
        )

    def dp_copy(peer):
        return pltpu.make_async_remote_copy(
            src_ref=red_dp.at[y], dst_ref=red_dp.at[y], send_sem=dp_send.at[peer], recv_sem=dp_recv.at[y],
            device_id={"dp": peer}, device_id_type=MESH,
        )

    def z_copy(peer):
        return pltpu.make_async_remote_copy(
            src_ref=red_z.at[z], dst_ref=red_z.at[z], send_sem=z_send.at[peer], recv_sem=z_recv.at[z],
            device_id={"tensor": peer}, device_id_type=MESH,
        )

    fin_copy = pltpu.make_async_remote_copy(
        src_ref=final, dst_ref=final, send_sem=fin_send, recv_sem=fin_recv,
        device_id={"pipe": 0}, device_id_type=MESH,
    )

    def collect():
        in_sum[...] = jnp.zeros_like(in_sum)

        @pl.loop(0, n)
        def _(s):
            arrived(in_low, low_recv, s)
            in_sum[...] += in_low[s].astype(jnp.float32)

        for m in range(micro):
            in_pad[m, :, taps:] = in_sum[:, m * seq : (m + 1) * seq]

        @pl.when(y < dps - 1)
        def _():
            halo_copy().start()

        @pl.when(y == 0)
        def _():
            in_pad[:, :, :taps] = jnp.zeros((micro, rank, taps), jnp.float32)

        for m in range(micro):
            each = parts // micro
            lower[m] = jnp.dot(
                in_pad[m, :, taps:], oc_ref[0, m * each : (m + 1) * each].reshape(seq, rank),
                precision=high, preferred_element_type=jnp.float32,
            )

    def turn():
        @pl.when(y > 0)
        def _():
            halo_copy().wait_recv()

        for m in range(micro):
            for b in range(seq // BLOCK):
                turned[m * (seq // BLOCK) + b] = lax.dot_general(
                    in_pad[m, :, b * BLOCK : (b + 1) * BLOCK + taps], back_ref[...], NT,
                    precision=high, preferred_element_type=jnp.float32,
                )

    @pl.when(jnp.logical_not(top))
    def _():
        for copy in saved_copies:
            copy.start()
        pl.semaphore_signal(barrier, inc=1, device_id={"pipe": 1}, device_id_type=MESH)
        pl.semaphore_wait(barrier, n)
        p0_copy.start()
        for copy in saved_copies:
            copy.wait()
        in_part()
        in_own[...] = in_sum[...].astype(jnp.bfloat16)

        @pl.loop(0, n)
        def _(s):
            low_copy(s).start()

        p0_copy.wait_send()

        @pl.loop(0, n)
        def _(s):
            low_copy(s).wait_send()

        fin_copy.wait_recv()
        out_ref[...] = final[:, :, :rank]

    @pl.when(top)
    def _():
        for r in range(parts):
            own_copy(r).start()
        p1_copy = pltpu.make_async_copy(po_hbm, p1, ls.at[2])

        @pl.loop(0, n)
        def _(s):
            pl.semaphore_signal(barrier, inc=1, device_id={"pipe": 0, "tensor": s}, device_id_type=MESH)

            @pl.when(s != z)
            def _():
                pl.semaphore_signal(barrier, inc=1, device_id={"tensor": s}, device_id_type=MESH)

        @pl.loop(0, dps)
        def _(s):
            @pl.when(s != y)
            def _():
                pl.semaphore_signal(barrier, inc=1, device_id={"dp": s}, device_id_type=MESH)

        pl.semaphore_wait(barrier, n + dps - 1)

        for g in range(pieces):
            @pl.when(has_left)
            def _():
                to_left(z, g, own_piece(g)).start()

            @pl.when(has_right)
            def _():
                to_right(z, g, own_piece(g)).start()

        p1_copy.start()
        for copy in saved_copies:
            copy.start()
        oc_ref[...] = jnp.zeros_like(oc_ref)
        upper[...] = jnp.zeros_like(upper)
        acc[...] = jnp.zeros_like(acc)
        for copy in saved_copies:
            copy.wait()
        in_part()
        in_up[...] = in_sum[...]

        @pl.loop(0, tiles)
        def _(c):
            cols = pl.ds(pl.multiple_of(c * tile, tile), tile)
            spec[0:2, :, cols] = jnp.dot(
                ftab_ref[...], fm_ref[:, cols], precision=lax.Precision.HIGHEST,
                preferred_element_type=jnp.float32,
            ).reshape(2, half, tile)
            for part in range(2):
                total = jnp.zeros((half, tile), jnp.float32)
                for j in range(fs_ref.shape[0]):
                    total += ftab_ref[part * half : (part + 1) * half, j : j + 1] * fs_ref[j, :, cols]
                spec[2 + part, :, cols] = total

        p1_copy.wait()
        p0_copy.wait_recv()
        for r in range(parts):
            own_copy(r).wait()
        oc_ref[0] = lax.dot_general(
            held[z].reshape(parts * BLOCK, width), p0[...], NT, preferred_element_type=jnp.float32
        ).reshape(parts, BLOCK, rank)
        multiply(z)
        if n < 3:
            collect()

        @pl.loop(1, n - 1)
        def _(k):
            from_left, from_right = z >= k, z + k < n

            @pl.when(k == n - 2)
            def _():
                collect()

            in_order = k == n - 2

            @pl.loop(0, pieces)
            def _(g):
                at_once = jnp.logical_or(jnp.logical_not(in_order), g < 2)

                @pl.when(from_left)
                def _():
                    to_right(z - k, g).wait_recv()

                    @pl.when(jnp.logical_and(has_right, at_once))
                    def _():
                        to_right(z - k, g).start()

                @pl.when(from_right)
                def _():
                    to_left(z + k, g).wait_recv()

                    @pl.when(jnp.logical_and(has_left, at_once))
                    def _():
                        to_left(z + k, g).start()

            @pl.when(from_left)
            def _():
                multiply(z - k)

            @pl.when(from_right)
            def _():
                multiply(z + k)

            @pl.when(in_order)
            def _():
                @pl.loop(2, pieces)
                def _(g):
                    @pl.when(jnp.logical_and(from_left, has_right))
                    def _():
                        to_right(z - k, g - 2).wait_send()
                        to_right(z - k, g).start()

                    @pl.when(jnp.logical_and(from_right, has_left))
                    def _():
                        to_left(z + k, g - 2).wait_send()
                        to_left(z + k, g).start()

        is_end = jnp.logical_or(z == 0, z == n - 1)
        farthest = n - 1 - z

        @pl.when(is_end)
        def _():
            weight_copy(farthest).start()

        turn()

        @pl.when(is_end)
        def _():
            weight_copy(farthest).wait()

        each = parts // micro

        @pl.loop(0, parts)
        def _(r):
            @pl.when(is_end)
            def _():
                to_left(farthest, 2 * r).wait_recv()
                to_left(farthest, 2 * r + 1).wait_recv()
                oc_ref[1, r] += lax.dot_general(
                    held[farthest, r], p1[:, shard_cols(farthest)], NT, preferred_element_type=jnp.float32
                )

            z_ref[...] = jnp.zeros_like(z_ref)
            span = pl.ds(pl.multiple_of(r * BLOCK, BLOCK), BLOCK)

            @pl.loop(0, tiles)
            def _(c):
                cols = pl.ds(pl.multiple_of(c * tile, tile), tile)

                @pl.when(is_end)
                def _():
                    acc[c, r] += lax.dot_general(
                        held[farthest, r], wbuf[cols, :], NT, preferred_element_type=jnp.float32
                    )

                back = acc[c, r].astype(jnp.bfloat16).astype(jnp.float32)
                gate_medium = (back * ss[span, cols].astype(jnp.float32)).astype(jnp.bfloat16)
                gate_short = (back * sm[span, cols].astype(jnp.float32)).astype(jnp.bfloat16)
                gm = jnp.dot(ahead_ref[...], gate_medium, preferred_element_type=jnp.float32)
                gs = jnp.dot(ahead_ref[...], gate_short, preferred_element_type=jnp.float32)
                m_re, m_im = spec[0, :, cols], spec[1, :, cols]
                s_re, s_im = spec[2, :, cols], spec[3, :, cols]
                real = m_re * gm[:half] - m_im * gm[half:] + s_re * gs[:half] - s_im * gs[half:]
                imag = m_re * gm[half:] + m_im * gm[:half] + s_re * gs[half:] + s_im * gs[:half]
                both = jnp.concatenate([real, imag], axis=0).astype(jnp.bfloat16)
                z_ref[...] += lax.dot_general(both, p0[:, cols], NT, preferred_element_type=jnp.float32)

            m = r // each
            lower[m] += jnp.dot(
                turned[r], z_ref[...], precision=high, preferred_element_type=jnp.float32
            )
            upper[m] += jnp.dot(
                in_up[:, span], oc_ref[1, r], precision=high, preferred_element_type=jnp.float32
            )

        for m in range(micro):
            red_dp[y, m] = jnp.concatenate([lower[m], upper[m]], axis=1) * scale

        @pl.loop(0, dps)
        def _(s):
            @pl.when(s != y)
            def _():
                dp_copy(s).start()

        @pl.loop(0, dps)
        def _(s):
            @pl.when(s != y)
            def _():
                arrived(red_dp, dp_recv, s)

        total = red_dp[0]
        for s in range(1, dps):
            total += red_dp[s]
        red_z[z] = total

        @pl.loop(0, n)
        def _(s):
            @pl.when(s != z)
            def _():
                z_copy(s).start()

        @pl.loop(0, n)
        def _(s):
            @pl.when(s != z)
            def _():
                arrived(red_z, z_recv, s)

        total = red_z[0]
        for s in range(1, n):
            total += red_z[s]
        final[...] = total
        fin_copy.start()
        out_ref[...] = final[:, :, rank:]
        fin_copy.wait_send()

        @pl.when(y < dps - 1)
        def _():
            halo_copy().wait_send()

        @pl.loop(0, dps)
        def _(s):
            @pl.when(s != y)
            def _():
                dp_copy(s).wait_send()

        @pl.loop(0, n)
        def _(s):
            @pl.when(s != z)
            def _():
                z_copy(s).wait_send()

            @pl.loop(0, pieces)
            def _(g):
                left = jnp.logical_and(has_left, s >= z)
                right = jnp.logical_and(has_right, s <= z)
                if n > 2:
                    left = jnp.logical_and(left, jnp.logical_or(s - z != n - 2, g >= pieces - 2))
                    right = jnp.logical_and(right, jnp.logical_or(z - s != n - 2, g >= pieces - 2))

                @pl.when(left)
                def _():
                    to_left(s, g).wait_send()

                @pl.when(right)
                def _():
                    to_right(s, g).wait_send()


def body(
    cotangent, saved_short, saved_medium, out_weight, short_filter, medium_filter, proj_in, proj_out
):
    n, dps = lax.axis_size("tensor"), lax.axis_size("dp")
    micro, seq, width = cotangent.shape
    rows = micro * seq
    channels = saved_short.shape[3]
    rank = proj_in.shape[2]
    taps = medium_filter.shape[1]
    ahead, ftab, back = transforms(taps)
    size = ahead.shape[0]
    tile = min(256, channels)
    parts = rows // BLOCK
    any_spec = pl.BlockSpec(memory_space=pl.ANY)
    vmem = pl.BlockSpec(memory_space=pltpu.VMEM)
    dma = pltpu.SemaphoreType.DMA
    low, full = jnp.bfloat16, jnp.float32
    grads = pl.pallas_call(
        functools.partial(kernel, n, tile),
        out_shape=jax.ShapeDtypeStruct((micro, rank, rank), full),
        in_specs=[any_spec] * 5 + [vmem] * 6,
        out_specs=vmem,
        scratch_shapes=[
            pltpu.VMEM((n, parts, BLOCK, width), low),
            pltpu.VMEM((channels // tile, parts, BLOCK, tile), full),
            pltpu.VMEM((channels, width), low),
            pltpu.VMEM((rows, channels), low),
            pltpu.VMEM((rows, channels), low),
            pltpu.VMEM((rank, width), low),
            pltpu.VMEM((rank, n * width), low),
            pltpu.VMEM((4, size // 2, channels), full),
            pltpu.VMEM((size, rank), full),
            pltpu.VMEM((2, parts, BLOCK, rank), full),
            pltpu.VMEM((rank, rows), low),
            pltpu.VMEM((rank, rows), full),
            pltpu.VMEM((n, rank, rows), low),
            pltpu.VMEM((rank, rows), full),
            pltpu.VMEM((micro, rank, taps + seq), full),
            pltpu.VMEM((parts, rank, size), full),
            pltpu.VMEM((micro, rank, rank), full),
            pltpu.VMEM((micro, rank, rank), full),
            pltpu.VMEM((dps, micro, rank, 2 * rank), full),
            pltpu.VMEM((n, micro, rank, 2 * rank), full),
            pltpu.VMEM((micro, rank, 2 * rank), full),
            dma((parts,)), dma, dma((3,)),
            dma((n, 2 * parts)), dma((n, 2 * parts)), dma((n, 2 * parts)),
            dma, dma,
            dma((n,)), dma((n,)), dma, dma,
            dma((dps,)), dma((dps,)), dma((n,)), dma((n,)), dma, dma,
        ],
        cost_estimate=pl.CostEstimate(
            flops=2 * rows * channels * width * n, bytes_accessed=2 * channels * width * n, transcendentals=0
        ),
        compiler_params=pltpu.CompilerParams(
            collective_id=0, has_side_effects=True, vmem_limit_bytes=60 * 2**20
        ),
        name="back_pass",
    )(
        cotangent.reshape(rows, width), out_weight[0], saved_short.reshape(rows, channels),
        saved_medium.reshape(rows, channels), proj_out[0].T, proj_in[0].T,
        medium_filter[0], short_filter.transpose(1, 0, 2), jnp.asarray(ahead), jnp.asarray(ftab), jnp.asarray(back),
    )
    return grads[None]


def solution(mesh):
    in_specs = (
        P(None, "dp", "tensor"),
        P("pipe", None, "dp", "tensor"),
        P("pipe", None, "dp", "tensor"),
        P("pipe", "tensor", None),
        P("pipe", None, "tensor"),
        P("pipe", None, "tensor"),
        P("pipe", "tensor", None),
        P("pipe", None, None),
    )
    out_specs = P("pipe", None, None, None)
    return jax.shard_map(body, mesh=mesh, in_specs=in_specs, out_specs=out_specs, check_vma=False)
```

```python
import functools
import math

import jax
import jax.numpy as jnp
import numpy as np
from jax import lax
from jax.experimental import pallas as pl
from jax.experimental.pallas import tpu as pltpu
from jax.sharding import PartitionSpec as P

MESH = pl.DeviceIdType.MESH
BLOCK = 256
NT = (((1,), (1,)), ((), ()))


def transforms(taps):
    size = BLOCK + taps
    freq = 2.0 * np.pi * (np.arange(size // 2) + 0.5) / size

    def table(times, sign):
        angle = freq[:, None] * times[None, :]
        return np.concatenate([np.cos(angle), sign * np.sin(angle)], axis=0)

    ahead = table(np.arange(BLOCK), -1.0).astype(jnp.bfloat16)
    filters = table(np.arange(taps), 1.0).astype(np.float32)
    back = (table(np.arange(-taps, BLOCK), -1.0) * (2.0 / size)).astype(np.float32)
    return ahead, filters, back


def kernel(
    n, tile,
    x_hbm, w_hbm, ss_hbm, sm_hbm, po_hbm, pi_ref, fm_ref, fs_ref, ahead_ref, ftab_ref, back_ref,
    out_ref,
    held, acc, wbuf, ss, sm, p0, p1, spec, z_ref, oc_ref,
    in_own, in_sum, in_low, in_up, in_full, in_pad, turned, lower, upper, red_dp, red_z, final,
    xs, ws, ls, send_l, send_r, recv, psend, precv,
    in_send, low_recv, halo_send, halo_recv,
    dp_send, dp_recv, z_send, z_recv, fin_send, fin_recv,
):
    z = lax.axis_index("tensor")
    y = lax.axis_index("dp")
    dps = red_dp.shape[0]
    micro, rank, padded = in_pad.shape
    parts, width = held.shape[1], held.shape[3]
    taps = padded - parts * BLOCK // micro
    seq = padded - taps
    scale = 1.0 / math.sqrt(seq * dps)
    high = lax.Precision.HIGHEST
    top = lax.axis_index("pipe") == lax.axis_size("pipe") - 1
    has_left, has_right = z > 0, z < n - 1
    half = spec.shape[1]
    tiles = spec.shape[2] // tile
    barrier = pltpu.get_barrier_semaphore()
    po_rows = pl.ds(pl.multiple_of(z * width, width), width)

    p0_copy = pltpu.make_async_remote_copy(
        src_ref=po_hbm.at[:, po_rows], dst_ref=p0, send_sem=psend, recv_sem=precv,
        device_id={"pipe": 1}, device_id_type=MESH,
    )

    def to_left(s, r, src=None):
        return pltpu.make_async_remote_copy(
            src_ref=held.at[s, r] if src is None else src, dst_ref=held.at[s, r],
            send_sem=send_l.at[s, r], recv_sem=recv.at[s, r],
            device_id={"tensor": z - 1}, device_id_type=MESH,
        )

    def to_right(s, r, src=None):
        return pltpu.make_async_remote_copy(
            src_ref=held.at[s, r] if src is None else src, dst_ref=held.at[s, r],
            send_sem=send_r.at[s, r], recv_sem=recv.at[s, r],
            device_id={"tensor": z + 1}, device_id_type=MESH,
        )

    def own_rows(r):
        return x_hbm.at[pl.ds(r * BLOCK, BLOCK), :]

    def own_copy(r):
        return pltpu.make_async_copy(own_rows(r), held.at[z, r], xs.at[r])

    def weight_copy(s):
        return pltpu.make_async_copy(
            w_hbm.at[:, pl.ds(pl.multiple_of(s * width, width), width)], wbuf, ws
        )

    def shard_cols(s):
        return pl.ds(pl.multiple_of(s * width, width), width)

    def multiply(s):
        weight_copy(s).start()
        shard = held[s].reshape(parts * BLOCK, width)
        oc_ref[1] += lax.dot_general(
            shard, p1[:, shard_cols(s)], NT, preferred_element_type=jnp.float32
        ).reshape(parts, BLOCK, rank)
        weight_copy(s).wait()

        @pl.loop(0, tiles)
        def _(c):
            weights = wbuf[pl.ds(pl.multiple_of(c * tile, tile), tile), :]
            acc[c] += lax.dot_general(
                held[s].reshape(parts * BLOCK, width), weights, NT, preferred_element_type=jnp.float32
            ).reshape(parts, BLOCK, tile)

    saved_copies = (
        pltpu.make_async_copy(ss_hbm, ss, ls.at[0]),
        pltpu.make_async_copy(sm_hbm, sm, ls.at[1]),
    )

    def in_part():
        in_sum[...] = jnp.zeros_like(in_sum)

        @pl.loop(0, tiles)
        def _(c):
            cols = pl.ds(pl.multiple_of(c * tile, tile), tile)
            gated = (ss[:, cols].astype(jnp.float32) * sm[:, cols].astype(jnp.float32)).astype(jnp.bfloat16)
            in_sum[...] += lax.dot_general(pi_ref[:, cols], gated, NT, preferred_element_type=jnp.float32)

    def chain_copy(way):
        return pltpu.make_async_remote_copy(
            src_ref=in_own.at[way], dst_ref=in_low.at[way], send_sem=in_send.at[way], recv_sem=low_recv.at[way],
            device_id={"tensor": z + 1 - 2 * way}, device_id_type=MESH,
        )

    full_copy = pltpu.make_async_remote_copy(
        src_ref=in_sum, dst_ref=in_full, send_sem=in_send.at[2], recv_sem=low_recv.at[2],
        device_id={"pipe": 1}, device_id_type=MESH,
    )

    def arrived(slots, sems, s):
        pltpu.make_async_copy(slots.at[s], slots.at[s], sems.at[s]).wait()

    def halo_copy():
        return pltpu.make_async_remote_copy(
            src_ref=in_pad.at[:, :, pl.ds(seq, taps)], dst_ref=in_pad.at[:, :, pl.ds(0, taps)],
            send_sem=halo_send, recv_sem=halo_recv, device_id={"dp": y + 1}, device_id_type=MESH,
        )

    def dp_copy(peer):
        return pltpu.make_async_remote_copy(
            src_ref=red_dp.at[y], dst_ref=red_dp.at[y], send_sem=dp_send.at[peer], recv_sem=dp_recv.at[y],
            device_id={"dp": peer}, device_id_type=MESH,
        )

    def z_copy(peer):
        return pltpu.make_async_remote_copy(
            src_ref=red_z.at[z], dst_ref=red_z.at[z], send_sem=z_send.at[peer], recv_sem=z_recv.at[z],
            device_id={"tensor": peer}, device_id_type=MESH,
        )

    fin_copy = pltpu.make_async_remote_copy(
        src_ref=final, dst_ref=final, send_sem=fin_send, recv_sem=fin_recv,
        device_id={"pipe": 0}, device_id_type=MESH,
    )

    def collect():
        full_copy.wait_recv()
        for m in range(micro):
            in_pad[m, :, taps:] = in_full[:, m * seq : (m + 1) * seq]

        @pl.when(y < dps - 1)
        def _():
            halo_copy().start()

        @pl.when(y == 0)
        def _():
            in_pad[:, :, :taps] = jnp.zeros((micro, rank, taps), jnp.float32)

        for m in range(micro):
            each = parts // micro
            lower[m] = jnp.dot(
                in_pad[m, :, taps:], oc_ref[0, m * each : (m + 1) * each].reshape(seq, rank),
                precision=high, preferred_element_type=jnp.float32,
            )

    def turn():
        @pl.when(y > 0)
        def _():
            halo_copy().wait_recv()

        for m in range(micro):
            for b in range(seq // BLOCK):
                turned[m * (seq // BLOCK) + b] = lax.dot_general(
                    in_pad[m, :, b * BLOCK : (b + 1) * BLOCK + taps], back_ref[...], NT,
                    precision=high, preferred_element_type=jnp.float32,
                )

    @pl.when(jnp.logical_not(top))
    def _():
        for copy in saved_copies:
            copy.start()
        pl.semaphore_signal(barrier, inc=1, device_id={"pipe": 1}, device_id_type=MESH)

        @pl.when(has_left)
        def _():
            pl.semaphore_signal(barrier, inc=1, device_id={"tensor": z - 1}, device_id_type=MESH)

        @pl.when(has_right)
        def _():
            pl.semaphore_signal(barrier, inc=1, device_id={"tensor": z + 1}, device_id_type=MESH)

        pl.semaphore_wait(barrier, 1 + jnp.minimum(z, 1) + jnp.minimum(n - 1 - z, 1))
        p0_copy.start()
        for copy in saved_copies:
            copy.wait()
        in_part()
        in_up[...] = in_sum[...]
        for way, (sends, takes) in enumerate(((has_right, has_left), (has_left, has_right))):
            @pl.when(jnp.logical_not(takes))
            def _():
                in_low[way] = jnp.zeros(in_low.shape[1:], jnp.bfloat16)

            @pl.when(takes)
            def _():
                chain_copy(way).wait_recv()

            @pl.when(sends)
            def _():
                in_own[way] = (in_up[...] + in_low[way].astype(jnp.float32)).astype(jnp.bfloat16)
                chain_copy(way).start()

            in_sum[...] += in_low[way].astype(jnp.float32)

        full_copy.start()
        p0_copy.wait_send()
        full_copy.wait_send()
        for way, sends in enumerate((has_right, has_left)):
            @pl.when(sends)
            def _():
                chain_copy(way).wait_send()

        fin_copy.wait_recv()
        out_ref[...] = final[:, :, :rank]

    @pl.when(top)
    def _():
        for r in range(parts):
            own_copy(r).start()
        p1_copy = pltpu.make_async_copy(po_hbm, p1, ls.at[2])

        pl.semaphore_signal(barrier, inc=1, device_id={"pipe": 0}, device_id_type=MESH)

        @pl.loop(0, n)
        def _(s):
            @pl.when(s != z)
            def _():
                pl.semaphore_signal(barrier, inc=1, device_id={"tensor": s}, device_id_type=MESH)

        @pl.loop(0, dps)
        def _(s):
            @pl.when(s != y)
            def _():
                pl.semaphore_signal(barrier, inc=1, device_id={"dp": s}, device_id_type=MESH)

        pl.semaphore_wait(barrier, n + dps - 1)

        for r in range(parts):
            @pl.when(has_left)
            def _():
                to_left(z, r, own_rows(r)).start()

            @pl.when(has_right)
            def _():
                to_right(z, r, own_rows(r)).start()

        p1_copy.start()
        for copy in saved_copies:
            copy.start()
        oc_ref[...] = jnp.zeros_like(oc_ref)
        upper[...] = jnp.zeros_like(upper)
        acc[...] = jnp.zeros_like(acc)
        for copy in saved_copies:
            copy.wait()
        in_part()
        in_up[...] = in_sum[...]

        @pl.loop(0, tiles)
        def _(c):
            cols = pl.ds(pl.multiple_of(c * tile, tile), tile)
            spec[0:2, :, cols] = jnp.dot(
                ftab_ref[...], fm_ref[:, cols], precision=lax.Precision.HIGHEST,
                preferred_element_type=jnp.float32,
            ).reshape(2, half, tile)
            for part in range(2):
                total = jnp.zeros((half, tile), jnp.float32)
                for j in range(fs_ref.shape[0]):
                    total += ftab_ref[part * half : (part + 1) * half, j : j + 1] * fs_ref[j, :, cols]
                spec[2 + part, :, cols] = total

        p1_copy.wait()
        p0_copy.wait_recv()
        for r in range(parts):
            own_copy(r).wait()
        oc_ref[0] = lax.dot_general(
            held[z].reshape(parts * BLOCK, width), p0[...], NT, preferred_element_type=jnp.float32
        ).reshape(parts, BLOCK, rank)
        multiply(z)
        if n < 3:
            collect()

        def forward(k, blocks):
            for r in blocks:
                @pl.when(z >= k)
                def _():
                    to_right(z - k, r).wait_recv()

                    @pl.when(has_right)
                    def _():
                        to_right(z - k, r).start()

                @pl.when(z + k < n)
                def _():
                    to_left(z + k, r).wait_recv()

                    @pl.when(has_left)
                    def _():
                        to_left(z + k, r).start()

        early, late = range(parts // 2), range(parts // 2, parts)
        if n > 2:
            forward(1, early)

        @pl.loop(1, n - 1)
        def _(k):
            forward(k, late)

            @pl.when(z >= k)
            def _():
                multiply(z - k)

            @pl.when(k < n - 2)
            def _():
                forward(k + 1, early)

            @pl.when(z + k < n)
            def _():
                multiply(z + k)

            @pl.when(k == n - 2)
            def _():
                collect()

        is_end = jnp.logical_or(z == 0, z == n - 1)
        farthest = n - 1 - z

        @pl.when(is_end)
        def _():
            weight_copy(farthest).start()

        turn()

        @pl.when(is_end)
        def _():
            weight_copy(farthest).wait()

        each = parts // micro

        @pl.loop(0, parts)
        def _(r):
            @pl.when(is_end)
            def _():
                to_left(farthest, r).wait_recv()
                oc_ref[1, r] += lax.dot_general(
                    held[farthest, r], p1[:, shard_cols(farthest)], NT, preferred_element_type=jnp.float32
                )

            z_ref[...] = jnp.zeros_like(z_ref)
            span = pl.ds(pl.multiple_of(r * BLOCK, BLOCK), BLOCK)

            @pl.loop(0, tiles)
            def _(c):
                cols = pl.ds(pl.multiple_of(c * tile, tile), tile)

                @pl.when(is_end)
                def _():
                    acc[c, r] += lax.dot_general(
                        held[farthest, r], wbuf[cols, :], NT, preferred_element_type=jnp.float32
                    )

                back = acc[c, r].astype(jnp.bfloat16).astype(jnp.float32)
                gate_medium = (back * ss[span, cols].astype(jnp.float32)).astype(jnp.bfloat16)
                gate_short = (back * sm[span, cols].astype(jnp.float32)).astype(jnp.bfloat16)
                gm = jnp.dot(ahead_ref[...], gate_medium, preferred_element_type=jnp.float32)
                gs = jnp.dot(ahead_ref[...], gate_short, preferred_element_type=jnp.float32)
                m_re, m_im = spec[0, :, cols], spec[1, :, cols]
                s_re, s_im = spec[2, :, cols], spec[3, :, cols]
                real = m_re * gm[:half] - m_im * gm[half:] + s_re * gs[:half] - s_im * gs[half:]
                imag = m_re * gm[half:] + m_im * gm[:half] + s_re * gs[half:] + s_im * gs[:half]
                both = jnp.concatenate([real, imag], axis=0).astype(jnp.bfloat16)
                z_ref[...] += lax.dot_general(both, p0[:, cols], NT, preferred_element_type=jnp.float32)

            m = r // each
            lower[m] += jnp.dot(
                turned[r], z_ref[...], precision=high, preferred_element_type=jnp.float32
            )
            upper[m] += jnp.dot(
                in_up[:, span], oc_ref[1, r], precision=high, preferred_element_type=jnp.float32
            )

        for m in range(micro):
            red_dp[y, m] = jnp.concatenate([lower[m], upper[m]], axis=1) * scale

        @pl.loop(0, dps)
        def _(s):
            @pl.when(s != y)
            def _():
                dp_copy(s).start()

        @pl.loop(0, dps)
        def _(s):
            @pl.when(s != y)
            def _():
                arrived(red_dp, dp_recv, s)

        total = red_dp[0]
        for s in range(1, dps):
            total += red_dp[s]
        red_z[z] = total

        @pl.loop(0, n)
        def _(s):
            @pl.when(s != z)
            def _():
                z_copy(s).start()

        @pl.loop(0, n)
        def _(s):
            @pl.when(s != z)
            def _():
                arrived(red_z, z_recv, s)

        total = red_z[0]
        for s in range(1, n):
            total += red_z[s]
        final[...] = total
        fin_copy.start()
        out_ref[...] = final[:, :, rank:]
        fin_copy.wait_send()

        @pl.when(y < dps - 1)
        def _():
            halo_copy().wait_send()

        @pl.loop(0, dps)
        def _(s):
            @pl.when(s != y)
            def _():
                dp_copy(s).wait_send()

        @pl.loop(0, n)
        def _(s):
            @pl.when(s != z)
            def _():
                z_copy(s).wait_send()

            @pl.loop(0, parts)
            def _(r):
                @pl.when(jnp.logical_and(has_left, s >= z))
                def _():
                    to_left(s, r).wait_send()

                @pl.when(jnp.logical_and(has_right, s <= z))
                def _():
                    to_right(s, r).wait_send()


def body(
    cotangent, saved_short, saved_medium, out_weight, short_filter, medium_filter, proj_in, proj_out
):
    n, dps = lax.axis_size("tensor"), lax.axis_size("dp")
    micro, seq, width = cotangent.shape
    rows = micro * seq
    channels = saved_short.shape[3]
    rank = proj_in.shape[2]
    taps = medium_filter.shape[1]
    ahead, ftab, back = transforms(taps)
    size = ahead.shape[0]
    tile = min(256, channels)
    parts = rows // BLOCK
    any_spec = pl.BlockSpec(memory_space=pl.ANY)
    vmem = pl.BlockSpec(memory_space=pltpu.VMEM)
    dma = pltpu.SemaphoreType.DMA
    low, full = jnp.bfloat16, jnp.float32
    grads = pl.pallas_call(
        functools.partial(kernel, n, tile),
        out_shape=jax.ShapeDtypeStruct((micro, rank, rank), full),
        in_specs=[any_spec] * 5 + [vmem] * 6,
        out_specs=vmem,
        scratch_shapes=[
            pltpu.VMEM((n, parts, BLOCK, width), low),
            pltpu.VMEM((channels // tile, parts, BLOCK, tile), full),
            pltpu.VMEM((channels, width), low),
            pltpu.VMEM((rows, channels), low),
            pltpu.VMEM((rows, channels), low),
            pltpu.VMEM((rank, width), low),
            pltpu.VMEM((rank, n * width), low),
            pltpu.VMEM((4, size // 2, channels), full),
            pltpu.VMEM((size, rank), full),
            pltpu.VMEM((2, parts, BLOCK, rank), full),
            pltpu.VMEM((2, rank, rows), low),
            pltpu.VMEM((rank, rows), full),
            pltpu.VMEM((2, rank, rows), low),
            pltpu.VMEM((rank, rows), full),
            pltpu.VMEM((rank, rows), full),
            pltpu.VMEM((micro, rank, taps + seq), full),
            pltpu.VMEM((parts, rank, size), full),
            pltpu.VMEM((micro, rank, rank), full),
            pltpu.VMEM((micro, rank, rank), full),
            pltpu.VMEM((dps, micro, rank, 2 * rank), full),
            pltpu.VMEM((n, micro, rank, 2 * rank), full),
            pltpu.VMEM((micro, rank, 2 * rank), full),
            dma((parts,)), dma, dma((3,)),
            dma((n, parts)), dma((n, parts)), dma((n, parts)),
            dma, dma,
            dma((3,)), dma((3,)), dma, dma,
            dma((dps,)), dma((dps,)), dma((n,)), dma((n,)), dma, dma,
        ],
        cost_estimate=pl.CostEstimate(
            flops=2 * rows * channels * width * n, bytes_accessed=2 * channels * width * n, transcendentals=0
        ),
        compiler_params=pltpu.CompilerParams(
            collective_id=0, has_side_effects=True, vmem_limit_bytes=60 * 2**20
        ),
        name="back_pass",
    )(
        cotangent.reshape(rows, width), out_weight[0], saved_short.reshape(rows, channels),
        saved_medium.reshape(rows, channels), proj_out[0].T, proj_in[0].T,
        medium_filter[0], short_filter.transpose(1, 0, 2), jnp.asarray(ahead), jnp.asarray(ftab), jnp.asarray(back),
    )
    return grads[None]


def solution(mesh):
    in_specs = (
        P(None, "dp", "tensor"),
        P("pipe", None, "dp", "tensor"),
        P("pipe", None, "dp", "tensor"),
        P("pipe", "tensor", None),
        P("pipe", None, "tensor"),
        P("pipe", None, "tensor"),
        P("pipe", "tensor", None),
        P("pipe", None, None),
    )
    out_specs = P("pipe", None, None, None)
    return jax.shard_map(body, mesh=mesh, in_specs=in_specs, out_specs=out_specs, check_vma=False)
```

```python
import functools
import math

import jax
import jax.numpy as jnp
import numpy as np
from jax import lax
from jax.experimental import pallas as pl
from jax.experimental.pallas import tpu as pltpu
from jax.sharding import PartitionSpec as P

MESH = pl.DeviceIdType.MESH
BLOCK = 256
NT = (((1,), (1,)), ((), ()))


def transforms(taps):
    size = BLOCK + taps
    freq = 2.0 * np.pi * (np.arange(size // 2) + 0.5) / size

    def table(times, sign):
        angle = freq[:, None] * times[None, :]
        return np.concatenate([np.cos(angle), sign * np.sin(angle)], axis=0)

    ahead = table(np.arange(BLOCK), -1.0).astype(jnp.bfloat16)
    filters = table(np.arange(taps), 1.0).astype(np.float32)
    back = (table(np.arange(-taps, BLOCK), -1.0) * (2.0 / size)).astype(np.float32)
    return ahead, filters, back


def kernel(
    n, tile,
    x_hbm, w_hbm, ss_hbm, sm_hbm, po_hbm, pi_ref, fm_ref, fs_ref, ahead_ref, ftab_ref, back_ref,
    out_ref,
    held, acc, wbuf, ss, sm, p0, p1, spec, z_ref, oc_ref,
    in_own, in_sum, in_low, in_up, in_full, in_pad, turned, lower, upper, red_dp, red_z, sums,
    xs, ws, ls, send_l, send_r, recv, psend, precv,
    in_send, low_recv, halo_send, halo_recv,
    dp_send, dp_recv, z_send, z_recv,
):
    z = lax.axis_index("tensor")
    y = lax.axis_index("dp")
    dps = red_dp.shape[0]
    micro, rank, padded = in_pad.shape
    parts, width = held.shape[1], held.shape[3]
    taps = padded - parts * BLOCK // micro
    seq = padded - taps
    scale = 1.0 / math.sqrt(seq * dps)
    high = lax.Precision.HIGHEST
    top = lax.axis_index("pipe") == lax.axis_size("pipe") - 1
    has_left, has_right = z > 0, z < n - 1
    half = spec.shape[1]
    tiles = spec.shape[2] // tile
    barrier = pltpu.get_barrier_semaphore()
    po_rows = pl.ds(pl.multiple_of(z * width, width), width)

    p0_copy = pltpu.make_async_remote_copy(
        src_ref=po_hbm.at[:, po_rows], dst_ref=p0, send_sem=psend, recv_sem=precv,
        device_id={"pipe": 1}, device_id_type=MESH,
    )

    def to_left(s, r, src=None):
        return pltpu.make_async_remote_copy(
            src_ref=held.at[s, r] if src is None else src, dst_ref=held.at[s, r],
            send_sem=send_l.at[s, r], recv_sem=recv.at[s, r],
            device_id={"tensor": z - 1}, device_id_type=MESH,
        )

    def to_right(s, r, src=None):
        return pltpu.make_async_remote_copy(
            src_ref=held.at[s, r] if src is None else src, dst_ref=held.at[s, r],
            send_sem=send_r.at[s, r], recv_sem=recv.at[s, r],
            device_id={"tensor": z + 1}, device_id_type=MESH,
        )

    def own_rows(r):
        return x_hbm.at[pl.ds(r * BLOCK, BLOCK), :]

    def own_copy(r):
        return pltpu.make_async_copy(own_rows(r), held.at[z, r], xs.at[r])

    def weight_copy(s):
        return pltpu.make_async_copy(
            w_hbm.at[:, pl.ds(pl.multiple_of(s * width, width), width)], wbuf, ws
        )

    def shard_cols(s):
        return pl.ds(pl.multiple_of(s * width, width), width)

    def multiply(s):
        weight_copy(s).start()
        shard = held[s].reshape(parts * BLOCK, width)
        oc_ref[1] += lax.dot_general(
            shard, p1[:, shard_cols(s)], NT, preferred_element_type=jnp.float32
        ).reshape(parts, BLOCK, rank)
        weight_copy(s).wait()

        @pl.loop(0, tiles)
        def _(c):
            weights = wbuf[pl.ds(pl.multiple_of(c * tile, tile), tile), :]
            acc[c] += lax.dot_general(
                held[s].reshape(parts * BLOCK, width), weights, NT, preferred_element_type=jnp.float32
            ).reshape(parts, BLOCK, tile)

    saved_copies = (
        pltpu.make_async_copy(ss_hbm, ss, ls.at[0]),
        pltpu.make_async_copy(sm_hbm, sm, ls.at[1]),
    )

    def in_part():
        in_sum[...] = jnp.zeros_like(in_sum)

        @pl.loop(0, tiles)
        def _(c):
            cols = pl.ds(pl.multiple_of(c * tile, tile), tile)
            gated = (ss[:, cols].astype(jnp.float32) * sm[:, cols].astype(jnp.float32)).astype(jnp.bfloat16)
            in_sum[...] += lax.dot_general(pi_ref[:, cols], gated, NT, preferred_element_type=jnp.float32)

    def chain_copy(way):
        return pltpu.make_async_remote_copy(
            src_ref=in_own.at[way], dst_ref=in_low.at[way], send_sem=in_send.at[way], recv_sem=low_recv.at[way],
            device_id={"tensor": z + 1 - 2 * way}, device_id_type=MESH,
        )

    full_copy = pltpu.make_async_remote_copy(
        src_ref=in_sum, dst_ref=in_full, send_sem=in_send.at[2], recv_sem=low_recv.at[2],
        device_id={"pipe": 1}, device_id_type=MESH,
    )

    def arrived(slots, sems, s):
        pltpu.make_async_copy(slots.at[s], slots.at[s], sems.at[s]).wait()

    def halo_copy():
        return pltpu.make_async_remote_copy(
            src_ref=in_pad.at[:, :, pl.ds(seq, taps)], dst_ref=in_pad.at[:, :, pl.ds(0, taps)],
            send_sem=halo_send, recv_sem=halo_recv, device_id={"dp": y + 1}, device_id_type=MESH,
        )

    def dp_copy(peer):
        return pltpu.make_async_remote_copy(
            src_ref=red_dp.at[y], dst_ref=red_dp.at[y], send_sem=dp_send.at[peer], recv_sem=dp_recv.at[y],
            device_id={"dp": peer}, device_id_type=MESH,
        )

    def z_copy(peer, pipe):
        return pltpu.make_async_remote_copy(
            src_ref=sums.at[pipe], dst_ref=red_z.at[z], send_sem=z_send.at[pipe, peer], recv_sem=z_recv.at[z],
            device_id={"pipe": pipe, "tensor": peer}, device_id_type=MESH,
        )

    def give():
        total = red_z[0]
        for s in range(1, n):
            total += red_z[s]
        for m in range(micro):
            out_ref[m] = total[:, m * rank : (m + 1) * rank]

    def collect():
        full_copy.wait_recv()
        for m in range(micro):
            in_pad[m, :, taps:] = in_full[:, m * seq : (m + 1) * seq]

        @pl.when(y < dps - 1)
        def _():
            halo_copy().start()

        @pl.when(y == 0)
        def _():
            in_pad[:, :, :taps] = jnp.zeros((micro, rank, taps), jnp.float32)

        for m in range(micro):
            each = parts // micro
            lower[m] = jnp.dot(
                in_pad[m, :, taps:], oc_ref[0, m * each : (m + 1) * each].reshape(seq, rank),
                precision=high, preferred_element_type=jnp.float32,
            )

    def turn():
        @pl.when(y > 0)
        def _():
            halo_copy().wait_recv()

        for m in range(micro):
            for b in range(seq // BLOCK):
                turned[m * (seq // BLOCK) + b] = lax.dot_general(
                    in_pad[m, :, b * BLOCK : (b + 1) * BLOCK + taps], back_ref[...], NT,
                    precision=high, preferred_element_type=jnp.float32,
                )

    @pl.when(jnp.logical_not(top))
    def _():
        for copy in saved_copies:
            copy.start()
        @pl.loop(0, n)
        def _(s):
            pl.semaphore_signal(barrier, inc=1, device_id={"pipe": 1, "tensor": s}, device_id_type=MESH)

        @pl.when(has_left)
        def _():
            pl.semaphore_signal(barrier, inc=1, device_id={"tensor": z - 1}, device_id_type=MESH)

        @pl.when(has_right)
        def _():
            pl.semaphore_signal(barrier, inc=1, device_id={"tensor": z + 1}, device_id_type=MESH)

        pl.semaphore_wait(barrier, n + jnp.minimum(z, 1) + jnp.minimum(n - 1 - z, 1))
        p0_copy.start()
        for copy in saved_copies:
            copy.wait()
        in_part()
        in_up[...] = in_sum[...]
        for way, (sends, takes) in enumerate(((has_right, has_left), (has_left, has_right))):
            @pl.when(jnp.logical_not(takes))
            def _():
                in_low[way] = jnp.zeros(in_low.shape[1:], jnp.bfloat16)

            @pl.when(takes)
            def _():
                chain_copy(way).wait_recv()

            @pl.when(sends)
            def _():
                in_own[way] = (in_up[...] + in_low[way].astype(jnp.float32)).astype(jnp.bfloat16)
                chain_copy(way).start()

            in_sum[...] += in_low[way].astype(jnp.float32)

        full_copy.start()
        p0_copy.wait_send()
        full_copy.wait_send()
        for way, sends in enumerate((has_right, has_left)):
            @pl.when(sends)
            def _():
                chain_copy(way).wait_send()

        @pl.loop(0, n)
        def _(s):
            arrived(red_z, z_recv, s)

        give()

    @pl.when(top)
    def _():
        for r in range(parts):
            own_copy(r).start()
        p1_copy = pltpu.make_async_copy(po_hbm, p1, ls.at[2])

        @pl.loop(0, n)
        def _(s):
            pl.semaphore_signal(barrier, inc=1, device_id={"pipe": 0, "tensor": s}, device_id_type=MESH)

            @pl.when(s != z)
            def _():
                pl.semaphore_signal(barrier, inc=1, device_id={"tensor": s}, device_id_type=MESH)

        @pl.loop(0, dps)
        def _(s):
            @pl.when(s != y)
            def _():
                pl.semaphore_signal(barrier, inc=1, device_id={"dp": s}, device_id_type=MESH)

        pl.semaphore_wait(barrier, 2 * n + dps - 2)

        for r in range(parts):
            @pl.when(has_left)
            def _():
                to_left(z, r, own_rows(r)).start()

            @pl.when(has_right)
            def _():
                to_right(z, r, own_rows(r)).start()

        p1_copy.start()
        for copy in saved_copies:
            copy.start()
        oc_ref[...] = jnp.zeros_like(oc_ref)
        upper[...] = jnp.zeros_like(upper)
        acc[...] = jnp.zeros_like(acc)
        for copy in saved_copies:
            copy.wait()
        in_part()
        in_up[...] = in_sum[...]

        @pl.loop(0, tiles)
        def _(c):
            cols = pl.ds(pl.multiple_of(c * tile, tile), tile)
            spec[0:2, :, cols] = jnp.dot(
                ftab_ref[...], fm_ref[:, cols], precision=lax.Precision.HIGHEST,
                preferred_element_type=jnp.float32,
            ).reshape(2, half, tile)
            for part in range(2):
                total = jnp.zeros((half, tile), jnp.float32)
                for j in range(fs_ref.shape[0]):
                    total += ftab_ref[part * half : (part + 1) * half, j : j + 1] * fs_ref[j, :, cols]
                spec[2 + part, :, cols] = total

        p1_copy.wait()
        p0_copy.wait_recv()
        for r in range(parts):
            own_copy(r).wait()
        oc_ref[0] = lax.dot_general(
            held[z].reshape(parts * BLOCK, width), p0[...], NT, preferred_element_type=jnp.float32
        ).reshape(parts, BLOCK, rank)
        multiply(z)
        if n < 3:
            collect()

        def forward(k, blocks):
            for r in blocks:
                @pl.when(z >= k)
                def _():
                    to_right(z - k, r).wait_recv()

                    @pl.when(has_right)
                    def _():
                        to_right(z - k, r).start()

                @pl.when(z + k < n)
                def _():
                    to_left(z + k, r).wait_recv()

                    @pl.when(has_left)
                    def _():
                        to_left(z + k, r).start()

        early, late = range(parts // 2), range(parts // 2, parts)
        if n > 2:
            forward(1, early)

        @pl.loop(1, n - 1)
        def _(k):
            forward(k, late)

            @pl.when(z >= k)
            def _():
                multiply(z - k)

            @pl.when(k < n - 2)
            def _():
                forward(k + 1, early)

            @pl.when(z + k < n)
            def _():
                multiply(z + k)

            @pl.when(k == n - 2)
            def _():
                collect()

        is_end = jnp.logical_or(z == 0, z == n - 1)
        farthest = n - 1 - z

        @pl.when(is_end)
        def _():
            weight_copy(farthest).start()

        turn()

        @pl.when(is_end)
        def _():
            weight_copy(farthest).wait()

        each = parts // micro

        @pl.loop(0, parts)
        def _(r):
            @pl.when(is_end)
            def _():
                to_left(farthest, r).wait_recv()
                oc_ref[1, r] += lax.dot_general(
                    held[farthest, r], p1[:, shard_cols(farthest)], NT, preferred_element_type=jnp.float32
                )

            z_ref[...] = jnp.zeros_like(z_ref)
            span = pl.ds(pl.multiple_of(r * BLOCK, BLOCK), BLOCK)

            @pl.loop(0, tiles)
            def _(c):
                cols = pl.ds(pl.multiple_of(c * tile, tile), tile)

                @pl.when(is_end)
                def _():
                    acc[c, r] += lax.dot_general(
                        held[farthest, r], wbuf[cols, :], NT, preferred_element_type=jnp.float32
                    )

                back = acc[c, r].astype(jnp.bfloat16).astype(jnp.float32)
                gate_medium = (back * ss[span, cols].astype(jnp.float32)).astype(jnp.bfloat16)
                gate_short = (back * sm[span, cols].astype(jnp.float32)).astype(jnp.bfloat16)
                gm = jnp.dot(ahead_ref[...], gate_medium, preferred_element_type=jnp.float32)
                gs = jnp.dot(ahead_ref[...], gate_short, preferred_element_type=jnp.float32)
                m_re, m_im = spec[0, :, cols], spec[1, :, cols]
                s_re, s_im = spec[2, :, cols], spec[3, :, cols]
                real = m_re * gm[:half] - m_im * gm[half:] + s_re * gs[:half] - s_im * gs[half:]
                imag = m_re * gm[half:] + m_im * gm[:half] + s_re * gs[half:] + s_im * gs[:half]
                both = jnp.concatenate([real, imag], axis=0).astype(jnp.bfloat16)
                z_ref[...] += lax.dot_general(both, p0[:, cols], NT, preferred_element_type=jnp.float32)

            m = r // each
            lower[m] += jnp.dot(
                turned[r], z_ref[...], precision=high, preferred_element_type=jnp.float32
            )
            upper[m] += jnp.dot(
                in_up[:, span], oc_ref[1, r], precision=high, preferred_element_type=jnp.float32
            )

        for i, part in enumerate((lower, upper)):
            red_dp[y, i] = jnp.concatenate([part[m] for m in range(micro)], axis=1) * scale

        @pl.loop(0, dps)
        def _(s):
            @pl.when(s != y)
            def _():
                dp_copy(s).start()

        @pl.loop(0, dps)
        def _(s):
            @pl.when(s != y)
            def _():
                arrived(red_dp, dp_recv, s)

        total = red_dp[0]
        for s in range(1, dps):
            total += red_dp[s]
        sums[...] = total
        red_z[z] = total[1]

        @pl.loop(0, n)
        def _(s):
            z_copy(s, 0).start()

            @pl.when(s != z)
            def _():
                z_copy(s, 1).start()

        @pl.loop(0, n)
        def _(s):
            @pl.when(s != z)
            def _():
                arrived(red_z, z_recv, s)

        give()

        @pl.when(y < dps - 1)
        def _():
            halo_copy().wait_send()

        @pl.loop(0, dps)
        def _(s):
            @pl.when(s != y)
            def _():
                dp_copy(s).wait_send()

        @pl.loop(0, n)
        def _(s):
            z_copy(s, 0).wait_send()

            @pl.when(s != z)
            def _():
                z_copy(s, 1).wait_send()

            @pl.loop(0, parts)
            def _(r):
                @pl.when(jnp.logical_and(has_left, s >= z))
                def _():
                    to_left(s, r).wait_send()

                @pl.when(jnp.logical_and(has_right, s <= z))
                def _():
                    to_right(s, r).wait_send()


def body(
    cotangent, saved_short, saved_medium, out_weight, short_filter, medium_filter, proj_in, proj_out
):
    n, dps = lax.axis_size("tensor"), lax.axis_size("dp")
    micro, seq, width = cotangent.shape
    rows = micro * seq
    channels = saved_short.shape[3]
    rank = proj_in.shape[2]
    taps = medium_filter.shape[1]
    ahead, ftab, back = transforms(taps)
    size = ahead.shape[0]
    tile = min(256, channels)
    parts = rows // BLOCK
    any_spec = pl.BlockSpec(memory_space=pl.ANY)
    vmem = pl.BlockSpec(memory_space=pltpu.VMEM)
    dma = pltpu.SemaphoreType.DMA
    low, full = jnp.bfloat16, jnp.float32
    grads = pl.pallas_call(
        functools.partial(kernel, n, tile),
        out_shape=jax.ShapeDtypeStruct((micro, rank, rank), full),
        in_specs=[any_spec] * 5 + [vmem] * 6,
        out_specs=vmem,
        scratch_shapes=[
            pltpu.VMEM((n, parts, BLOCK, width), low),
            pltpu.VMEM((channels // tile, parts, BLOCK, tile), full),
            pltpu.VMEM((channels, width), low),
            pltpu.VMEM((rows, channels), low),
            pltpu.VMEM((rows, channels), low),
            pltpu.VMEM((rank, width), low),
            pltpu.VMEM((rank, n * width), low),
            pltpu.VMEM((4, size // 2, channels), full),
            pltpu.VMEM((size, rank), full),
            pltpu.VMEM((2, parts, BLOCK, rank), full),
            pltpu.VMEM((2, rank, rows), low),
            pltpu.VMEM((rank, rows), full),
            pltpu.VMEM((2, rank, rows), low),
            pltpu.VMEM((rank, rows), full),
            pltpu.VMEM((rank, rows), full),
            pltpu.VMEM((micro, rank, taps + seq), full),
            pltpu.VMEM((parts, rank, size), full),
            pltpu.VMEM((micro, rank, rank), full),
            pltpu.VMEM((micro, rank, rank), full),
            pltpu.VMEM((dps, 2, rank, micro * rank), full),
            pltpu.VMEM((n, rank, micro * rank), full),
            pltpu.VMEM((2, rank, micro * rank), full),
            dma((parts,)), dma, dma((3,)),
            dma((n, parts)), dma((n, parts)), dma((n, parts)),
            dma, dma,
            dma((3,)), dma((3,)), dma, dma,
            dma((dps,)), dma((dps,)), dma((2, n)), dma((n,)),
        ],
        cost_estimate=pl.CostEstimate(
            flops=2 * rows * channels * width * n, bytes_accessed=2 * channels * width * n, transcendentals=0
        ),
        compiler_params=pltpu.CompilerParams(
            collective_id=0, has_side_effects=True, vmem_limit_bytes=60 * 2**20
        ),
        name="back_pass",
    )(
        cotangent.reshape(rows, width), out_weight[0], saved_short.reshape(rows, channels),
        saved_medium.reshape(rows, channels), proj_out[0].T, proj_in[0].T,
        medium_filter[0], short_filter.transpose(1, 0, 2), jnp.asarray(ahead), jnp.asarray(ftab), jnp.asarray(back),
    )
    return grads[None]


def solution(mesh):
    in_specs = (
        P(None, "dp", "tensor"),
        P("pipe", None, "dp", "tensor"),
        P("pipe", None, "dp", "tensor"),
        P("pipe", "tensor", None),
        P("pipe", None, "tensor"),
        P("pipe", None, "tensor"),
        P("pipe", "tensor", None),
        P("pipe", None, None),
    )
    out_specs = P("pipe", None, None, None)
    return jax.shard_map(body, mesh=mesh, in_specs=in_specs, out_specs=out_specs, check_vma=False)
```
